32 devices in a mesh: tm: 16 (over z, y, x), head: 2 (over core).
Axes of the slice: x: 2, y: 2, z: 4, core: 2. Of those that a mesh axis runs over, the one named last changes fastest.
Arguments:
- queries: bfloat16 [2048, 4096], P('tm', 'head'), may hold values from -6 to 6
- keys: bfloat16 [2048, 4096], P('tm', 'head'), may hold values from -6 to 6
- values: bfloat16 [2048, 4096], P('tm', 'head'), may hold values from -6 to 6
- log_decay: float32 [32, 2048], P('head', 'tm'), may hold values from -1 to 0
- agent_ids: int32 [2048], P('tm'), may hold values from 0 to 127
- norm_gain: float32 [4096], P('head'), may hold values from 0.1 to 1.9
- out_grad: bfloat16 [2048, 4096], P('tm', 'head'), may hold values from -6 to 6
Outputs:
- result: bfloat16 [2048, 4096], P('tm', 'head')
- query_grad: bfloat16 [2048, 4096], P('tm', 'head')
- key_grad: bfloat16 [2048, 4096], P('tm', 'head')
- value_grad: bfloat16 [2048, 4096], P('tm', 'head')
- decay_grad: float32 [32, 2048], P('head', 'tm')
- gain_grad: float32 [4096], P('head')
The draws below stay inside these ranges and needn't reach their ends.
All inputs are finite; a program needn't handle non-finite values.
Results may differ from the reference program's by a relative error of at most 0.001.
Values sent between devices are 32-bit elements; how exact they have to be, the bound alone decides.
A program may use at most 128 MiB of HBM per device.

```python
import math
import jax
import jax.numpy as jnp
from jax import lax

ATTENTION_GROUPS = 32
DK = 128
GROUP = 128
AGENTS = 128
TEAM = 16
WIDTH = 4096
SEQUENCE_STEPS = 2048


def draw_log_decay(key, part):
    number_of_pieces = jax.random.split(key, 7)
    fast = jax.random.uniform(number_of_pieces[1], (ATTENTION_GROUPS, 1)) < 0.4
    slow_rate = jnp.exp(jax.random.uniform(number_of_pieces[0], (ATTENTION_GROUPS, 1), minval=math.log(1e-06), maxval=math.log(1e-05)))
    fast_rate = jnp.exp(jax.random.uniform(number_of_pieces[2], (ATTENTION_GROUPS, 1), minval=math.log(0.012), maxval=math.log(0.025)))
    starting_position = jnp.where(fast, fast_rate, slow_rate)
    approximate_guess = jax.random.uniform(number_of_pieces[3], (ATTENTION_GROUPS, SEQUENCE_STEPS), minval=0.3, maxval=3.0)
    window_width = jnp.exp(jax.random.uniform(number_of_pieces[4], (ATTENTION_GROUPS, SEQUENCE_STEPS // GROUP, 1), minval=math.log(0.5), maxval=math.log(2.0)))
    window_width = jnp.broadcast_to(window_width, (ATTENTION_GROUPS, SEQUENCE_STEPS // GROUP, GROUP)).reshape(ATTENTION_GROUPS, SEQUENCE_STEPS)
    segment_extent = jax.random.uniform(number_of_pieces[5], (ATTENTION_GROUPS, SEQUENCE_STEPS)) < 3.0 / SEQUENCE_STEPS
    sequence_steps_total = jax.random.uniform(number_of_pieces[6], (ATTENTION_GROUPS, SEQUENCE_STEPS), minval=0.22, maxval=0.69)
    return (-(starting_position * approximate_guess * window_width + jnp.where(segment_extent, sequence_steps_total, 0.0))).astype(jnp.float32)


def place_ends(entries, rng, least, top_value):
    longest = entries.shape.index(max(entries.shape))
    spots = []
    for shift in (0, 1):
        where = [jax.random.randint(jax.random.fold_in(rng, axis), (), 0, length) for axis, length in enumerate(entries.shape)]
        where[longest] = (where[longest] + shift) % entries.shape[longest]
        spots.append(tuple(where))
    return entries.at[spots[0]].set(least).at[spots[1]].set(top_value)


def level_of(own_key, dims, cuts, smallest, top_value):
    level, own = 1.0, jax.random.fold_in(own_key, 6)
    for axis_at, shards_of in cuts:
        steps = jnp.exp(jax.random.uniform(jax.random.fold_in(own, axis_at), (shards_of,), jnp.float32, smallest / len(cuts), top_value / len(cuts)))
        level = level * jnp.repeat(steps, dims[axis_at] // shards_of).reshape([-1 if axis == axis_at else 1 for axis in range(len(dims))])
    return level


def noise(key, shape, width, reach, pieces=(), dtype=jnp.bfloat16):
    loudness = level_of(key, shape, pieces, -0.22, 0.18) if pieces else 1.0
    array = jax.random.normal(key, shape, jnp.float32) * width * loudness
    return jnp.minimum(jnp.maximum(array, -reach), reach).astype(dtype)


def setup_inputs(seed: int = 0) -> dict:
    seeds = jax.random.split(jax.random.key(seed), 8)
    return {
        "queries": noise(seeds[0], (SEQUENCE_STEPS, WIDTH), 1.0, 6.0, ((0, 16), (1, 2))),
        "keys": noise(seeds[1], (SEQUENCE_STEPS, WIDTH), 1.0, 6.0, ((0, 16), (1, 2))),
        "values": noise(seeds[2], (SEQUENCE_STEPS, WIDTH), 1.0, 6.0, ((0, 16), (1, 2))),
        "log_decay": draw_log_decay(jax.random.fold_in(seeds[7], 71), 0),
        "agent_ids": place_ends(jax.random.randint(seeds[4], (SEQUENCE_STEPS,), 0, AGENTS), jax.random.fold_in(seeds[4], 1), 0, AGENTS - 1).astype(jnp.int32),
        "norm_gain": jnp.clip(1.0 + 0.18 * jax.random.normal(seeds[5], (WIDTH,), jnp.float32), 0.1, 1.9),
        "out_grad": noise(seeds[6], (SEQUENCE_STEPS, WIDTH), 1.0, 6.0, ((0, 16), (1, 2))),
    }


EPS = 1e-06
HIGH = lax.Precision.HIGHEST

def group_pass(scaled, key_rows, value_rows, decays, teams):
    length, heads, depth = scaled.shape
    blocks = length // GROUP
    query_blocks = scaled.reshape(blocks, GROUP, heads, depth)
    key_blocks = key_rows.reshape(blocks, GROUP, heads, depth)
    value_blocks = value_rows.reshape(blocks, GROUP, heads, depth)
    decay_blocks = decays.reshape(heads, blocks, GROUP).transpose(1, 0, 2)
    team_blocks = teams.reshape(blocks, GROUP)
    places = jnp.arange(GROUP)
    causal = places[:, None] >= places[None, :]

    def advance(state, inputs):
        query_block, key_block, value_block, decay_block, team_block = inputs
        cumulative = jnp.cumsum(decay_block, axis=1)
        visible = (causal & (team_block[:, None] == team_block[None, :]))[None]
        spread = cumulative[:, :, None] - cumulative[:, None, :]
        weights = jnp.where(visible, jnp.exp(jnp.where(visible, spread, 0.0)), 0.0)
        scores = jnp.einsum('thd,shd->hts', query_block, key_block, precision=HIGH) * weights
        output = jnp.einsum('hts,she->the', scores, value_block, precision=HIGH)
        carried = jnp.einsum('thd,hde->the', query_block, state, precision=HIGH)
        output = output + jnp.exp(cumulative).T[:, :, None] * carried
        tail = jnp.exp(cumulative[:, -1:] - cumulative)
        fresh = jnp.einsum('shd,she->hde', key_block * tail.T[:, :, None], value_block, precision=HIGH)
        state = jnp.exp(cumulative[:, -1])[:, None, None] * state + fresh
        return (state, output)
    start = jnp.zeros((heads, depth, depth), jnp.float32)
    final, outputs = lax.scan(advance, start, (query_blocks, key_blocks, value_blocks, decay_blocks, team_blocks))
    return (outputs.reshape(length, heads, depth), final)

def layer(query_in, key_in, value_in, decays, gain, teams):
    length = query_in.shape[0]
    scaled = query_in.reshape(length, ATTENTION_GROUPS, DK) * DK ** (-0.5)
    output, final = group_pass(scaled, key_in.reshape(length, ATTENTION_GROUPS, DK), value_in.reshape(length, ATTENTION_GROUPS, DK), decays, teams)
    flat = output.reshape(length, WIDTH)
    rms_value = jnp.sqrt(lax.optimization_barrier(jnp.mean(flat * flat, axis=1)) + EPS)
    return flat / rms_value[:, None] * gain

def reference(queries, keys, values, log_decay, agent_ids, norm_gain, out_grad):
    teams = agent_ids // TEAM

    def forward(query_in, key_in, value_in, decays, gain):
        return layer(query_in, key_in, value_in, decays, gain, teams)
    output, pullback = jax.vjp(forward, queries.astype(jnp.float32), keys.astype(jnp.float32), values.astype(jnp.float32), log_decay, norm_gain)
    query_g, key_g, value_g, decay_g, gain_g = pullback(out_grad.astype(jnp.float32))
    return (output.astype(jnp.bfloat16), query_g.astype(jnp.bfloat16), key_g.astype(jnp.bfloat16), value_g.astype(jnp.bfloat16), decay_g, gain_g)
```

```python
import functools
import math

import jax
import jax.numpy as jnp
from jax import lax
from jax.experimental import pallas as pl
from jax.experimental.pallas import tpu as pltpu
from jax.sharding import PartitionSpec as P

DK = 128
TEAM = 16
EPS = 1e-06
UNROLL = 2
MESH = pl.DeviceIdType.MESH
F32, BF16 = jnp.float32, jnp.bfloat16
NN, NT, TN = ((1,), (0,)), ((1,), (1,)), ((0,), (0,))


def split(value, count=2):
    parts = []
    for _ in range(count):
        part = value.astype(BF16)
        parts.append(part)
        value = value - part.astype(F32)
    return tuple(parts)


def product(left, right, form):
    order = max(len(left), len(right))
    pairs = [(a, b) for i, a in enumerate(left) for j, b in enumerate(right) if i + j < order]
    lefts = jnp.concatenate([a for a, _ in pairs], axis=form[0][0])
    rights = jnp.concatenate([b for _, b in pairs], axis=form[1][0])
    return lax.dot_general(lefts, rights, (form, ((), ())), preferred_element_type=F32)


class Scan:
    def __init__(self, back, group, chain, share, refs, factors, sems, chain_sems):
        self.back, self.group, self.chain, self.share = back, group, chain, share
        self.own, self.dealt, self.came, self.gone, self.given, self.got = refs
        self.factors, self.sems, self.chain_sems = factors, sems, chain_sems
        me = lax.axis_index("tm")
        self.inner, self.outer = lax.rem(me, group), lax.div(me, group)
        self.sent = []

    def peer(self, step):
        return lax.rem(self.inner + step, self.group)

    def copy(self, source, target, send, receive, outer, inner):
        return pltpu.make_async_remote_copy(
            src_ref=source,
            dst_ref=target,
            send_sem=send,
            recv_sem=receive,
            device_id={"tm": outer * self.group + inner},
            device_id_type=MESH,
        )

    def deal_copy(self, step, chunk):
        peer = self.peer(step)
        sems = self.sems.at[0, :, step - 1, chunk]
        return self.copy(
            self.own.at[peer * self.share + chunk],
            self.dealt.at[self.inner, chunk],
            sems.at[0],
            sems.at[1],
            self.outer,
            peer,
        )

    def give_copy(self, step, chunk):
        peer = self.peer(step)
        sems = self.sems.at[1, :, step - 1, chunk]
        return self.copy(
            self.given.at[peer, chunk],
            self.got.at[self.inner * self.share + chunk],
            sems.at[0],
            sems.at[1],
            self.outer,
            peer,
        )

    def chain_copy(self, chunk):
        outer = self.outer + (-1 if self.back else 1)
        outer = lax.rem(outer + self.chain, self.chain)
        sems = self.chain_sems
        return self.copy(
            self.gone.at[chunk],
            self.came.at[chunk],
            sems.at[0, chunk],
            sems.at[1, chunk],
            outer,
            self.inner,
        )

    def first(self):
        return self.outer == (self.chain - 1 if self.back else 0)

    def last(self):
        return self.outer == (0 if self.back else self.chain - 1)

    def deal(self, chunk):
        for step in range(1, self.group):
            self.deal_copy(step, chunk).start()
        self.dealt[self.inner, chunk] = self.own[self.inner * self.share + chunk]

    def combine(self, chunk):
        for step in range(1, self.group):
            self.deal_copy(step, chunk).wait_recv()
        order = range(self.group)
        row = pl.ds(self.inner * self.share + chunk, 1)
        passed, through = None, []
        for place in reversed(order) if self.back else order:
            through.append((place, passed))
            factor = self.factors[place, row, :]
            term = self.dealt[place, chunk]
            if passed is None:
                total, passed = term, factor
                self.given[place, chunk] = jnp.zeros_like(term)
            else:
                self.given[place, chunk] = total
                total, passed = total * factor + term, passed * factor
        if self.chain > 1:

            @pl.when(self.first())
            def _():
                self.came[chunk] = jnp.zeros_like(total)

            @pl.when(jnp.logical_not(self.first()))
            def _():
                self.chain_copy(chunk).wait_recv()

            before = self.came[chunk]
            self.gone[chunk] = before * passed + total

            @pl.when(jnp.logical_not(self.last()))
            def _():
                self.chain_copy(chunk).start()

            for place, factor in through:
                added = before if factor is None else before * factor
                self.given[place, chunk] += added
        for step in range(1, self.group):
            self.give_copy(step, chunk).start()
        self.got[self.inner * self.share + chunk] = self.given[self.inner, chunk]

    def arrive(self, chunk):
        for step in range(1, self.group):
            self.give_copy(step, chunk).wait_recv()

    def finish(self):
        for chunk in range(self.share):
            for step in range(1, self.group):
                self.deal_copy(step, chunk).wait_send()
                self.give_copy(step, chunk).wait_send()
            if self.chain > 1:

                @pl.when(jnp.logical_not(self.last()))
                def _():
                    self.chain_copy(chunk).wait_send()


def kernel(
    group, chain, split_heads,
    q_ref, k_ref, v_ref, decay_ref, agent_ref, gain_ref, grad_ref,
    y_ref, q_grad_ref, k_grad_ref, v_grad_ref, decay_grad_ref, gain_grad_ref,
    sum_ref, total_ref, spread_ref, bias_ref, factor_ref, score_ref, weight_ref, out_ref, adjoint_ref,
    k_part_ref, v_part_ref, norm_ref, scale_ref, change_ref, gain_ref_in, gain_ref_out,
    end_ref, dealt_ref, came_ref, gone_ref, given_ref, state_ref,
    start_ref, dealt_back_ref, came_back_ref, gone_back_ref, given_back_ref, later_ref,
    scan_sems, chain_sems, factor_sems, norm_sems, gain_sems_in, gain_sems_out,
):
    length, width = q_ref.shape
    heads = width // DK
    share = heads // group
    scale = DK**-0.5
    full_width = width * split_heads
    me, side = lax.axis_index("tm"), lax.axis_index("head")
    inner, outer = lax.rem(me, group), lax.div(me, group)

    inner_peers = [outer * group + lax.rem(inner + step, group) for step in range(1, group)]
    outer_peers = [lax.rem(outer + step, chain) * group + inner for step in range(1, chain)]
    side_peers = [lax.rem(side + step, split_heads) for step in range(1, split_heads)]

    barrier = pltpu.get_barrier_semaphore()
    for peer in inner_peers + outer_peers:
        pl.semaphore_signal(barrier, inc=1, device_id={"tm": peer}, device_id_type=MESH)
    for peer in side_peers:
        pl.semaphore_signal(barrier, inc=1, device_id={"head": peer}, device_id_type=MESH)

    def to_peers(ref, place, peers, axis, sems):
        return [
            pltpu.make_async_remote_copy(
                src_ref=ref.at[place],
                dst_ref=ref.at[place],
                send_sem=sems.at[0, number],
                recv_sem=sems.at[1, number],
                device_id={axis: peer},
                device_id_type=MESH,
            )
            for number, peer in enumerate(peers)
        ]

    forward = Scan(
        False, group, chain, share,
        (end_ref, dealt_ref, came_ref, gone_ref, given_ref, state_ref),
        factor_ref, scan_sems.at[0], chain_sems.at[0],
    )
    backward = Scan(
        True, group, chain, share,
        (start_ref, dealt_back_ref, came_back_ref, gone_back_ref, given_back_ref, later_ref),
        factor_ref, scan_sems.at[1], chain_sems.at[1],
    )

    def columns(head):
        return pl.ds(pl.multiple_of(head * DK, DK), DK)

    def row(head):
        return pl.ds(head, 1)

    def each_head(chunk, work):
        def step(place, carry):
            work(place * share + chunk)
            return carry

        lax.fori_loop(0, group, step, None, unroll=UNROLL)

    rows_at = lax.broadcasted_iota(jnp.int32, (length, length), 0)
    lanes_at = lax.broadcasted_iota(jnp.int32, (length, length), 1)
    decays = split(decay_ref[...], 3)
    up_to = jnp.where(rows_at <= lanes_at, 1.0, 0.0).astype(BF16)
    sum_ref[...] = product(decays, (up_to,), NN)
    total_ref[...] = product(decays, (jnp.ones((length, DK), BF16),), NN)
    factor_ref[inner] = jnp.exp(total_ref[...])
    teams = jnp.broadcast_to(lax.div(agent_ref[...], TEAM).astype(F32), (length, length))
    visible = (rows_at >= lanes_at) & (teams == teams.T)
    bias_ref[...] = jnp.where(visible, 0.0, -1e30)

    def own_end(head):
        across = jnp.broadcast_to(sum_ref[row(head), :], (length, length))
        down = across.T
        spread_ref[head] = down
        tail = jnp.exp(total_ref[row(head), :] - down)
        keys = k_ref[:, columns(head)].astype(F32) * tail
        end_ref[head] = product(split(keys), (v_ref[:, columns(head)],), TN)

    each_head(0, own_end)
    pl.semaphore_wait(barrier, len(inner_peers) + len(outer_peers) + len(side_peers))
    factor_copies = to_peers(factor_ref, inner, inner_peers, "tm", factor_sems)
    for copy in factor_copies:
        copy.start()
    forward.deal(0)
    for chunk in range(1, share):
        each_head(chunk, own_end)
        forward.deal(chunk)

    def own_out(head):
        across = sum_ref[row(head), :]
        weight = jnp.exp(spread_ref[head] - across + bias_ref[...])
        weight_ref[head] = weight
        score = product((q_ref[:, columns(head)],), (k_ref[:, columns(head)],), NT) * weight * scale
        score_ref[head] = score
        out_ref[head] = product(split(score), (v_ref[:, columns(head)],), NN)

    for copy in factor_copies:
        copy.wait_recv()
    for chunk in range(share):
        each_head(chunk, own_out)
        forward.combine(chunk)

    norm_ref[side] = jnp.zeros_like(norm_ref[side])

    def whole_out(head):
        reached = product((q_ref[:, columns(head)],), split(state_ref[head]), NN)
        out = out_ref[head] + jnp.exp(spread_ref[head]) * scale * reached
        out_ref[head] = out
        gained = grad_ref[:, columns(head)].astype(F32) * gain_ref[row(head), :]
        norm_ref[side, 0] += out * out
        norm_ref[side, 1] += gained * out

    for chunk in range(share):
        forward.arrive(chunk)
        each_head(chunk, whole_out)

    norm_copies = to_peers(norm_ref, side, side_peers, "head", norm_sems)
    for copy in norm_copies:
        copy.start()
    for copy in norm_copies:
        copy.wait_recv()
    squares, inners = norm_ref[0, 0], norm_ref[0, 1]
    for place in range(1, split_heads):
        squares, inners = squares + norm_ref[place, 0], inners + norm_ref[place, 1]
    rms = jnp.sqrt(jnp.sum(squares, axis=1, keepdims=True) / full_width + EPS)
    bent = jnp.sum(inners, axis=1, keepdims=True) / (full_width * rms * rms * rms)
    scale_ref[0] = jnp.broadcast_to(1.0 / rms, (length, DK))
    scale_ref[1] = jnp.broadcast_to(bent, (length, DK))

    def own_start(head):
        grads = grad_ref[:, columns(head)].astype(F32)
        gain = gain_ref[row(head), :]
        out = out_ref[head]
        normed = out * scale_ref[0]
        adjoint = grads * gain * scale_ref[0] - out * scale_ref[1]
        adjoint_ref[head] = adjoint
        weighted = adjoint * jnp.exp(spread_ref[head]) * scale
        start_ref[head] = product((q_ref[:, columns(head)],), split(weighted), TN)
        y_ref[:, columns(head)] = (normed * gain).astype(BF16)
        gain_ref_in[inner, row(head), :] = jnp.sum(grads * normed, axis=0, keepdims=True)

    for chunk in range(share):
        each_head(chunk, own_start)
        backward.deal(chunk)
    gain_copies_in = to_peers(gain_ref_in, inner, inner_peers, "tm", gain_sems_in)
    for copy in gain_copies_in:
        copy.start()

    def own_grads(head):
        queries, keys = q_ref[:, columns(head)], k_ref[:, columns(head)]
        adjoint = split(adjoint_ref[head])
        pairs = split(product(adjoint, (v_ref[:, columns(head)],), NT) * weight_ref[head])
        reached = product(adjoint, split(state_ref[head]), NT) * jnp.exp(spread_ref[head])
        q_grad = (product(pairs, (keys,), NN) + reached) * scale
        q_grad_ref[:, columns(head)] = q_grad.astype(BF16)
        k_part_ref[head] = product(pairs, (queries,), TN) * scale
        v_part_ref[head] = product(split(score_ref[head]), adjoint, TN)

    for chunk in range(share):
        each_head(chunk, own_grads)
        backward.combine(chunk)

    for copy in gain_copies_in:
        copy.wait_recv()
    gain_sum = gain_ref_in[0]
    for place in range(1, group):
        gain_sum = gain_sum + gain_ref_in[place]
    gain_ref_out[outer] = gain_sum
    gain_copies_out = to_peers(gain_ref_out, outer, outer_peers, "tm", gain_sems_out)
    for copy in gain_copies_out:
        copy.start()

    ones = jnp.ones((16, DK), BF16)
    ends_here = rows_at == length - 1

    def whole_grads(head):
        later = later_ref[head]
        parts = split(later)
        keys = k_ref[:, columns(head)]
        tail = jnp.exp(total_ref[row(head), :] - spread_ref[head])
        k_grad = k_part_ref[head] + tail * product((v_ref[:, columns(head)],), parts, NT)
        v_grad = v_part_ref[head] + tail * product((keys,), parts, NN)
        k_grad_ref[:, columns(head)] = k_grad.astype(BF16)
        v_grad_ref[:, columns(head)] = v_grad.astype(BF16)
        after = state_ref[head] * jnp.exp(total_ref[row(head), :]) + end_ref[head]
        at_end = jnp.sum(after * later, axis=0, keepdims=True)
        change = out_ref[head] * adjoint_ref[head] - keys.astype(F32) * k_grad
        change = change + jnp.where(ends_here, at_end, 0.0)
        change_ref[row(head), :] = product((ones,), split(change, 3), NT)[:1]

    for chunk in range(share):
        backward.arrive(chunk)
        each_head(chunk, whole_grads)
    from_here = jnp.where(rows_at >= lanes_at, 1.0, 0.0).astype(BF16)
    decay_grad_ref[...] = product(split(change_ref[...], 3), (from_here,), NN)

    for copy in gain_copies_out:
        copy.wait_recv()
    gain_sum = gain_ref_out[0]
    for place in range(1, chain):
        gain_sum = gain_sum + gain_ref_out[place]
    gain_grad_ref[...] = gain_sum

    forward.finish()
    backward.finish()
    for copy in factor_copies + norm_copies + gain_copies_in + gain_copies_out:
        copy.wait_send()


def body(group, chain, split_heads, queries, keys, values, log_decay, agent_ids, norm_gain, out_grad):
    length, width = queries.shape
    heads = width // DK
    share = heads // group
    state = (DK, DK)
    row_shape = (heads, DK)
    travelling = [
        pltpu.VMEM((heads, *state), F32),
        pltpu.VMEM((group, share, *state), F32),
        pltpu.VMEM((share, *state), F32),
        pltpu.VMEM((share, *state), F32),
        pltpu.VMEM((group, share, *state), F32),
        pltpu.VMEM((heads, *state), F32),
    ]
    per_head = pltpu.VMEM((heads, length, DK), F32)
    peers, others, sides = max(1, group - 1), max(1, chain - 1), max(1, split_heads - 1)
    wide = jax.ShapeDtypeStruct((length, width), BF16)
    outs = pl.pallas_call(
        functools.partial(kernel, group, chain, split_heads),
        out_shape=[
            wide,
            wide,
            wide,
            wide,
            jax.ShapeDtypeStruct((heads, length), F32),
            jax.ShapeDtypeStruct((heads, DK), F32),
        ],
        in_specs=[pl.BlockSpec(memory_space=pltpu.VMEM)] * 7,
        out_specs=[pl.BlockSpec(memory_space=pltpu.VMEM)] * 6,
        scratch_shapes=[
            pltpu.VMEM(row_shape, F32),
            pltpu.VMEM(row_shape, F32),
            per_head,
            pltpu.VMEM((length, length), F32),
            pltpu.VMEM((group, *row_shape), F32),
            per_head,
            per_head,
            per_head,
            per_head,
            per_head,
            per_head,
            pltpu.VMEM((split_heads, 2, length, DK), F32),
            pltpu.VMEM((2, length, DK), F32),
            pltpu.VMEM(row_shape, F32),
            pltpu.VMEM((group, *row_shape), F32),
            pltpu.VMEM((chain, *row_shape), F32),
            *travelling,
            *travelling,
            pltpu.SemaphoreType.DMA((2, 2, 2, peers, share)),
            pltpu.SemaphoreType.DMA((2, 2, share)),
            pltpu.SemaphoreType.DMA((2, peers)),
            pltpu.SemaphoreType.DMA((2, sides)),
            pltpu.SemaphoreType.DMA((2, peers)),
            pltpu.SemaphoreType.DMA((2, others)),
        ],
        compiler_params=pltpu.CompilerParams(
            collective_id=0, has_side_effects=True, vmem_limit_bytes=48 * 2**20
        ),
        cost_estimate=pl.CostEstimate(
            flops=heads * 28 * 2 * DK**3,
            bytes_accessed=8 * length * width * 2,
            transcendentals=heads * 5 * DK**2,
        ),
    )(
        queries,
        keys,
        values,
        log_decay,
        agent_ids.reshape(1, length),
        norm_gain.reshape(heads, DK),
        out_grad,
    )
    return (*outs[:5], outs[5].reshape(width))


def solution(mesh):
    count, split_heads = mesh.shape["tm"], mesh.shape["head"]

    def placed_body(queries, *rest):
        group = math.gcd(math.gcd(count, queries.shape[1] // DK), 4)
        return body(group, count // group, split_heads, queries, *rest)

    wide = P("tm", "head")
    return jax.shard_map(
        placed_body,
        mesh=mesh,
        in_specs=(wide, wide, wide, P("head", "tm"), P("tm"), P("head"), wide),
        out_specs=(wide, wide, wide, wide, P("head", "tm"), P("head")),
        check_vma=False,
    )
```

```python
import functools
import math

import jax
import jax.numpy as jnp
from jax import lax
from jax.experimental import pallas as pl
from jax.experimental.pallas import tpu as pltpu
from jax.sharding import PartitionSpec as P

DK = 128
TEAM = 16
EPS = 1e-06
UNROLL = 4
MESH = pl.DeviceIdType.MESH
F32, BF16 = jnp.float32, jnp.bfloat16
NN, NT, TN = ((1,), (0,)), ((1,), (1,)), ((0,), (0,))


def split(value, count=2):
    parts = []
    for _ in range(count):
        part = value.astype(BF16)
        parts.append(part)
        value = value - part.astype(F32)
    return tuple(parts)


def product(left, right, form):
    order = max(len(left), len(right))
    pairs = [(a, b) for i, a in enumerate(left) for j, b in enumerate(right) if i + j < order]
    lefts = jnp.concatenate([a for a, _ in pairs], axis=form[0][0])
    rights = jnp.concatenate([b for _, b in pairs], axis=form[1][0])
    return lax.dot_general(lefts, rights, (form, ((), ())), preferred_element_type=F32)


class Scan:
    def __init__(self, back, group, chain, share, refs, factors, sems, chain_sems):
        self.back, self.group, self.chain, self.share = back, group, chain, share
        self.own, self.dealt, self.came, self.gone, self.given, self.got = refs
        self.factors, self.sems, self.chain_sems = factors, sems, chain_sems
        me = lax.axis_index("tm")
        self.inner, self.outer = lax.rem(me, group), lax.div(me, group)
        self.sent = []

    def peer(self, step):
        return lax.rem(self.inner + step, self.group)

    def copy(self, source, target, send, receive, outer, inner):
        return pltpu.make_async_remote_copy(
            src_ref=source,
            dst_ref=target,
            send_sem=send,
            recv_sem=receive,
            device_id={"tm": outer * self.group + inner},
            device_id_type=MESH,
        )

    def deal_copy(self, step, chunk):
        peer = self.peer(step)
        sems = self.sems.at[0, :, step - 1, chunk]
        return self.copy(
            self.own.at[peer * self.share + chunk],
            self.dealt.at[self.inner, chunk],
            sems.at[0],
            sems.at[1],
            self.outer,
            peer,
        )

    def give_copy(self, step, chunk):
        peer = self.peer(step)
        sems = self.sems.at[1, :, step - 1, chunk]
        return self.copy(
            self.given.at[peer, chunk],
            self.got.at[self.inner * self.share + chunk],
            sems.at[0],
            sems.at[1],
            self.outer,
            peer,
        )

    def chain_copy(self, chunk):
        outer = self.outer + (-1 if self.back else 1)
        outer = lax.rem(outer + self.chain, self.chain)
        sems = self.chain_sems
        return self.copy(
            self.gone.at[chunk],
            self.came.at[chunk],
            sems.at[0, chunk],
            sems.at[1, chunk],
            outer,
            self.inner,
        )

    def first(self):
        return self.outer == (self.chain - 1 if self.back else 0)

    def last(self):
        return self.outer == (0 if self.back else self.chain - 1)

    def deal(self, chunk):
        for step in range(1, self.group):
            self.deal_copy(step, chunk).start()
        self.dealt[self.inner, chunk] = self.own[self.inner * self.share + chunk]

    def combine(self, chunk):
        for step in range(1, self.group):
            self.deal_copy(step, chunk).wait_recv()
        order = range(self.group)
        row = pl.ds(self.inner * self.share + chunk, 1)
        passed, through = None, []
        for place in reversed(order) if self.back else order:
            through.append((place, passed))
            factor = self.factors[place, row, :]
            term = self.dealt[place, chunk]
            if passed is None:
                total, passed = term, factor
                self.given[place, chunk] = jnp.zeros_like(term)
            else:
                self.given[place, chunk] = total
                total, passed = total * factor + term, passed * factor
        if self.chain > 1:

            @pl.when(self.first())
            def _():
                self.came[chunk] = jnp.zeros_like(total)

            @pl.when(jnp.logical_not(self.first()))
            def _():
                self.chain_copy(chunk).wait_recv()

            before = self.came[chunk]
            self.gone[chunk] = before * passed + total

            @pl.when(jnp.logical_not(self.last()))
            def _():
                self.chain_copy(chunk).start()

            for place, factor in through:
                added = before if factor is None else before * factor
                self.given[place, chunk] += added
        for step in range(1, self.group):
            self.give_copy(step, chunk).start()
        self.got[self.inner * self.share + chunk] = self.given[self.inner, chunk]

    def arrive(self, chunk):
        for step in range(1, self.group):
            self.give_copy(step, chunk).wait_recv()

    def finish(self):
        for chunk in range(self.share):
            for step in range(1, self.group):
                self.deal_copy(step, chunk).wait_send()
                self.give_copy(step, chunk).wait_send()
            if self.chain > 1:

                @pl.when(jnp.logical_not(self.last()))
                def _():
                    self.chain_copy(chunk).wait_send()


def kernel(
    group, chain, split_heads,
    q_from, k_from, v_from, decay_from, agent_from, gain_from, grad_from,
    y_ref, q_grad_ref, k_grad_ref, v_grad_ref, decay_grad_ref, gain_grad_ref,
    q_ref, k_ref, v_ref, decay_ref, agent_ref, gain_ref, grad_ref,
    sum_ref, total_ref, spread_ref, bias_ref, factor_ref, score_ref, weight_ref, out_ref, adjoint_ref,
    k_part_ref, v_part_ref, norm_ref, scale_ref, change_ref, gain_ref_in, gain_ref_out,
    end_ref, dealt_ref, came_ref, gone_ref, given_ref, state_ref,
    start_ref, dealt_back_ref, came_back_ref, gone_back_ref, given_back_ref, later_ref,
    load_sems, scan_sems, chain_sems, factor_sems, norm_sems, gain_sems_in, gain_sems_out,
):
    loads = [
        pltpu.make_async_copy(source, target, load_sems.at[number])
        for number, (source, target) in enumerate(
            [
                (decay_from, decay_ref),
                (k_from, k_ref),
                (v_from, v_ref),
                (q_from, q_ref),
                (agent_from, agent_ref),
                (gain_from, gain_ref),
                (grad_from, grad_ref),
            ]
        )
    ]
    for load in loads:
        load.start()
    length, width = q_ref.shape
    heads = width // DK
    share = heads // group
    scale = DK**-0.5
    full_width = width * split_heads
    me, side = lax.axis_index("tm"), lax.axis_index("head")
    inner, outer = lax.rem(me, group), lax.div(me, group)

    inner_peers = [outer * group + lax.rem(inner + step, group) for step in range(1, group)]
    outer_peers = [lax.rem(outer + step, chain) * group + inner for step in range(1, chain)]
    side_peers = [lax.rem(side + step, split_heads) for step in range(1, split_heads)]

    barrier = pltpu.get_barrier_semaphore()
    for peer in inner_peers + outer_peers:
        pl.semaphore_signal(barrier, inc=1, device_id={"tm": peer}, device_id_type=MESH)
    for peer in side_peers:
        pl.semaphore_signal(barrier, inc=1, device_id={"head": peer}, device_id_type=MESH)

    def to_peers(ref, place, peers, axis, sems):
        return [
            pltpu.make_async_remote_copy(
                src_ref=ref.at[place],
                dst_ref=ref.at[place],
                send_sem=sems.at[0, number],
                recv_sem=sems.at[1, number],
                device_id={axis: peer},
                device_id_type=MESH,
            )
            for number, peer in enumerate(peers)
        ]

    forward = Scan(
        False, group, chain, share,
        (end_ref, dealt_ref, came_ref, gone_ref, given_ref, state_ref),
        factor_ref, scan_sems.at[0], chain_sems.at[0],
    )
    backward = Scan(
        True, group, chain, share,
        (start_ref, dealt_back_ref, came_back_ref, gone_back_ref, given_back_ref, later_ref),
        factor_ref, scan_sems.at[1], chain_sems.at[1],
    )

    def columns(head):
        return pl.ds(pl.multiple_of(head * DK, DK), DK)

    def row(head):
        return pl.ds(head, 1)

    def each_head(chunk, work):
        def step(place, carry):
            work(place * share + chunk)
            return carry

        lax.fori_loop(0, group, step, None, unroll=UNROLL)

    rows_at = lax.broadcasted_iota(jnp.int32, (length, length), 0)
    lanes_at = lax.broadcasted_iota(jnp.int32, (length, length), 1)
    loads[0].wait()
    decays = split(decay_ref[...], 3)
    up_to = jnp.where(rows_at <= lanes_at, 1.0, 0.0).astype(BF16)
    sum_ref[...] = product(decays, (up_to,), NN)
    total_ref[...] = product(decays, (jnp.ones((length, DK), BF16),), NN)
    factor_ref[inner] = jnp.exp(total_ref[...])

    def own_end(head):
        across = jnp.broadcast_to(sum_ref[row(head), :], (length, length))
        down = across.T
        spread_ref[head] = down
        tail = jnp.exp(total_ref[row(head), :] - down)
        keys = k_ref[:, columns(head)].astype(F32) * tail
        end_ref[head] = product(split(keys), (v_ref[:, columns(head)],), TN)

    for load in loads[1:3]:
        load.wait()
    each_head(0, own_end)
    pl.semaphore_wait(barrier, len(inner_peers) + len(outer_peers) + len(side_peers))
    factor_copies = to_peers(factor_ref, inner, inner_peers, "tm", factor_sems)
    for copy in factor_copies:
        copy.start()
    forward.deal(0)
    for chunk in range(1, share):
        each_head(chunk, own_end)
        forward.deal(chunk)

    for load in loads[3:]:
        load.wait()
    teams = jnp.broadcast_to(lax.div(agent_ref[...], TEAM).astype(F32), (length, length))
    visible = (rows_at >= lanes_at) & (teams == teams.T)
    bias_ref[...] = jnp.where(visible, 0.0, -1e30)

    def own_out(head):
        across = sum_ref[row(head), :]
        weight = jnp.exp(spread_ref[head] - across + bias_ref[...])
        weight_ref[head] = weight
        score = product((q_ref[:, columns(head)],), (k_ref[:, columns(head)],), NT) * weight * scale
        score_ref[head] = score
        out_ref[head] = product(split(score), (v_ref[:, columns(head)],), NN)

    for copy in factor_copies:
        copy.wait_recv()
    for chunk in range(share):
        forward.combine(chunk)
        each_head(chunk, own_out)

    norm_ref[side] = jnp.zeros_like(norm_ref[side])

    def whole_out(head):
        reached = product((q_ref[:, columns(head)],), split(state_ref[head]), NN)
        out = out_ref[head] + jnp.exp(spread_ref[head]) * scale * reached
        out_ref[head] = out
        gained = grad_ref[:, columns(head)].astype(F32) * gain_ref[row(head), :]
        norm_ref[side, 0] += out * out
        norm_ref[side, 1] += gained * out

    for chunk in range(share):
        forward.arrive(chunk)
        each_head(chunk, whole_out)

    norm_copies = to_peers(norm_ref, side, side_peers, "head", norm_sems)
    for copy in norm_copies:
        copy.start()
    for copy in norm_copies:
        copy.wait_recv()
    squares, inners = norm_ref[0, 0], norm_ref[0, 1]
    for place in range(1, split_heads):
        squares, inners = squares + norm_ref[place, 0], inners + norm_ref[place, 1]
    rms = jnp.sqrt(jnp.sum(squares, axis=1, keepdims=True) / full_width + EPS)
    bent = jnp.sum(inners, axis=1, keepdims=True) / (full_width * rms * rms * rms)
    scale_ref[0] = jnp.broadcast_to(1.0 / rms, (length, DK))
    scale_ref[1] = jnp.broadcast_to(bent, (length, DK))

    def own_start(head):
        gained = grad_ref[:, columns(head)].astype(F32) * gain_ref[row(head), :]
        adjoint = gained * scale_ref[0] - out_ref[head] * scale_ref[1]
        adjoint_ref[head] = adjoint
        weighted = adjoint * jnp.exp(spread_ref[head]) * scale
        start_ref[head] = product((q_ref[:, columns(head)],), split(weighted), TN)

    for chunk in range(share):
        each_head(chunk, own_start)
        backward.deal(chunk)

    def result(head):
        normed = out_ref[head] * scale_ref[0]
        y_ref[:, columns(head)] = (normed * gain_ref[row(head), :]).astype(BF16)
        grads = grad_ref[:, columns(head)].astype(F32)
        gain_ref_in[inner, row(head), :] = jnp.sum(grads * normed, axis=0, keepdims=True)

    for chunk in range(share):
        each_head(chunk, result)
    gain_copies_in = to_peers(gain_ref_in, inner, inner_peers, "tm", gain_sems_in)
    for copy in gain_copies_in:
        copy.start()

    def own_grads(head):
        queries, keys = q_ref[:, columns(head)], k_ref[:, columns(head)]
        adjoint = split(adjoint_ref[head])
        pairs = split(product(adjoint, (v_ref[:, columns(head)],), NT) * weight_ref[head])
        reached = product(adjoint, split(state_ref[head]), NT) * jnp.exp(spread_ref[head])
        q_grad = (product(pairs, (keys,), NN) + reached) * scale
        q_grad_ref[:, columns(head)] = q_grad.astype(BF16)
        k_part_ref[head] = product(pairs, (queries,), TN) * scale
        v_part_ref[head] = product(split(score_ref[head]), adjoint, TN)

    for chunk in range(share):
        backward.combine(chunk)
        each_head(chunk, own_grads)

    for copy in gain_copies_in:
        copy.wait_recv()
    gain_sum = gain_ref_in[0]
    for place in range(1, group):
        gain_sum = gain_sum + gain_ref_in[place]
    gain_ref_out[outer] = gain_sum
    gain_copies_out = to_peers(gain_ref_out, outer, outer_peers, "tm", gain_sems_out)
    for copy in gain_copies_out:
        copy.start()

    ones = jnp.ones((16, DK), BF16)
    ends_here = rows_at == length - 1

    def whole_grads(head):
        later = later_ref[head]
        parts = split(later)
        keys = k_ref[:, columns(head)]
        tail = jnp.exp(total_ref[row(head), :] - spread_ref[head])
        k_grad = k_part_ref[head] + tail * product((v_ref[:, columns(head)],), parts, NT)
        v_grad = v_part_ref[head] + tail * product((keys,), parts, NN)
        k_grad_ref[:, columns(head)] = k_grad.astype(BF16)
        v_grad_ref[:, columns(head)] = v_grad.astype(BF16)
        after = state_ref[head] * jnp.exp(total_ref[row(head), :]) + end_ref[head]
        at_end = jnp.sum(after * later, axis=0, keepdims=True)
        change = out_ref[head] * adjoint_ref[head] - keys.astype(F32) * k_grad
        change = change + jnp.where(ends_here, at_end, 0.0)
        change_ref[row(head), :] = product((ones,), split(change, 3), NT)[:1]

    for chunk in range(share):
        backward.arrive(chunk)
        each_head(chunk, whole_grads)
    from_here = jnp.where(rows_at >= lanes_at, 1.0, 0.0).astype(BF16)
    decay_grad_ref[...] = product(split(change_ref[...], 3), (from_here,), NN)

    for copy in gain_copies_out:
        copy.wait_recv()
    gain_sum = gain_ref_out[0]
    for place in range(1, chain):
        gain_sum = gain_sum + gain_ref_out[place]
    gain_grad_ref[...] = gain_sum

    forward.finish()
    backward.finish()
    for copy in factor_copies + norm_copies + gain_copies_in + gain_copies_out:
        copy.wait_send()


def writer(*refs):
    *arrays, sems = refs
    half = len(arrays) // 2
    copies = [
        pltpu.make_async_copy(source, target, sems.at[number])
        for number, (source, target) in enumerate(zip(arrays[:half], arrays[half:]))
    ]
    for copy in copies:
        copy.start()
    for copy in copies:
        copy.wait()


def body(group, chain, split_heads, queries, keys, values, log_decay, agent_ids, norm_gain, out_grad):
    length, width = queries.shape
    heads = width // DK
    share = heads // group
    state = (DK, DK)
    row_shape = (heads, DK)
    travelling = [
        pltpu.VMEM((heads, *state), F32),
        pltpu.VMEM((group, share, *state), F32),
        pltpu.VMEM((share, *state), F32),
        pltpu.VMEM((share, *state), F32),
        pltpu.VMEM((group, share, *state), F32),
        pltpu.VMEM((heads, *state), F32),
    ]
    per_head = pltpu.VMEM((heads, length, DK), F32)
    peers, others, sides = max(1, group - 1), max(1, chain - 1), max(1, split_heads - 1)
    wide = jax.ShapeDtypeStruct((length, width), BF16)
    outs = pl.pallas_call(
        functools.partial(kernel, group, chain, split_heads),
        out_shape=[
            wide,
            wide,
            wide,
            wide,
            jax.ShapeDtypeStruct((heads, length), F32),
            jax.ShapeDtypeStruct((heads, DK), F32),
        ],
        in_specs=[pl.BlockSpec(memory_space=pltpu.HBM)] * 7,
        out_specs=[pl.BlockSpec(memory_space=pltpu.VMEM)] * 6,
        scratch_shapes=[
            *[pltpu.VMEM((length, width), BF16)] * 3,
            pltpu.VMEM((heads, length), F32),
            pltpu.VMEM((1, length), agent_ids.dtype),
            pltpu.VMEM(row_shape, F32),
            pltpu.VMEM((length, width), BF16),
            pltpu.VMEM(row_shape, F32),
            pltpu.VMEM(row_shape, F32),
            per_head,
            pltpu.VMEM((length, length), F32),
            pltpu.VMEM((group, *row_shape), F32),
            per_head,
            per_head,
            per_head,
            per_head,
            per_head,
            per_head,
            pltpu.VMEM((split_heads, 2, length, DK), F32),
            pltpu.VMEM((2, length, DK), F32),
            pltpu.VMEM(row_shape, F32),
            pltpu.VMEM((group, *row_shape), F32),
            pltpu.VMEM((chain, *row_shape), F32),
            *travelling,
            *travelling,
            pltpu.SemaphoreType.DMA((7,)),
            pltpu.SemaphoreType.DMA((2, 2, 2, peers, share)),
            pltpu.SemaphoreType.DMA((2, 2, share)),
            pltpu.SemaphoreType.DMA((2, peers)),
            pltpu.SemaphoreType.DMA((2, sides)),
            pltpu.SemaphoreType.DMA((2, peers)),
            pltpu.SemaphoreType.DMA((2, others)),
        ],
        compiler_params=pltpu.CompilerParams(
            collective_id=0, has_side_effects=True, vmem_limit_bytes=48 * 2**20
        ),
        cost_estimate=pl.CostEstimate(
            flops=heads * 28 * 2 * DK**3,
            bytes_accessed=8 * length * width * 2,
            transcendentals=heads * 5 * DK**2,
        ),
    )(
        queries,
        keys,
        values,
        log_decay,
        agent_ids.reshape(1, length),
        norm_gain.reshape(heads, DK),
        out_grad,
    )
    outs = pl.pallas_call(
        writer,
        out_shape=[jax.ShapeDtypeStruct(out.shape, out.dtype) for out in outs],
        in_specs=[pl.BlockSpec(memory_space=pltpu.VMEM)] * 6,
        out_specs=[pl.BlockSpec(memory_space=pltpu.HBM)] * 6,
        scratch_shapes=[pltpu.SemaphoreType.DMA((6,))],
    )(*outs)
    return (*outs[:5], outs[5].reshape(width))


def solution(mesh):
    count, split_heads = mesh.shape["tm"], mesh.shape["head"]

    def placed_body(queries, *rest):
        group = math.gcd(math.gcd(count, queries.shape[1] // DK), 4)
        return body(group, count // group, split_heads, queries, *rest)

    wide = P("tm", "head")
    return jax.shard_map(
        placed_body,
        mesh=mesh,
        in_specs=(wide, wide, wide, P("head", "tm"), P("tm"), P("head"), wide),
        out_specs=(wide, wide, wide, wide, P("head", "tm"), P("head")),
        check_vma=False,
    )
```

```python
import functools
import math

import jax
import jax.numpy as jnp
from jax import lax
from jax.experimental import pallas as pl
from jax.experimental.pallas import tpu as pltpu
from jax.sharding import PartitionSpec as P

DK = 128
TEAM = 16
EPS = 1e-06
UNROLL = 4
MESH = pl.DeviceIdType.MESH
F32, BF16 = jnp.float32, jnp.bfloat16
NN, NT, TN = ((1,), (0,)), ((1,), (1,)), ((0,), (0,))


def split(value, count=2):
    parts = []
    for _ in range(count):
        part = value.astype(BF16)
        parts.append(part)
        value = value - part.astype(F32)
    return tuple(parts)


def product(left, right, form):
    order = max(len(left), len(right))
    pairs = [(a, b) for i, a in enumerate(left) for j, b in enumerate(right) if i + j < order]
    lefts = jnp.concatenate([a for a, _ in pairs], axis=form[0][0])
    rights = jnp.concatenate([b for _, b in pairs], axis=form[1][0])
    return lax.dot_general(lefts, rights, (form, ((), ())), preferred_element_type=F32)


class Scan:
    def __init__(self, back, group, chain, share, refs, factors, sems, chain_sems):
        self.back, self.group, self.chain, self.share = back, group, chain, share
        self.own, self.dealt, self.came, self.gone, self.given, self.got = refs
        self.factors, self.sems, self.chain_sems = factors, sems, chain_sems
        me = lax.axis_index("tm")
        self.inner, self.outer = lax.rem(me, group), lax.div(me, group)
        self.sent = []

    def peer(self, step):
        return lax.rem(self.inner + step, self.group)

    def copy(self, source, target, send, receive, outer, inner):
        return pltpu.make_async_remote_copy(
            src_ref=source,
            dst_ref=target,
            send_sem=send,
            recv_sem=receive,
            device_id={"tm": outer * self.group + inner},
            device_id_type=MESH,
        )

    def deal_copy(self, step, chunk):
        peer = self.peer(step)
        sems = self.sems.at[0, :, step - 1, chunk]
        return self.copy(
            self.own.at[peer * self.share + chunk],
            self.dealt.at[self.inner, chunk],
            sems.at[0],
            sems.at[1],
            self.outer,
            peer,
        )

    def give_copy(self, step, chunk):
        peer = self.peer(step)
        sems = self.sems.at[1, :, step - 1, chunk]
        return self.copy(
            self.given.at[peer, chunk],
            self.got.at[self.inner * self.share + chunk],
            sems.at[0],
            sems.at[1],
            self.outer,
            peer,
        )

    def chain_copy(self, chunk):
        outer = self.outer + (-1 if self.back else 1)
        outer = lax.rem(outer + self.chain, self.chain)
        sems = self.chain_sems
        return self.copy(
            self.gone.at[chunk],
            self.came.at[chunk],
            sems.at[0, chunk],
            sems.at[1, chunk],
            outer,
            self.inner,
        )

    def first(self):
        return self.outer == (self.chain - 1 if self.back else 0)

    def last(self):
        return self.outer == (0 if self.back else self.chain - 1)

    def deal(self, chunk):
        for step in range(1, self.group):
            self.deal_copy(step, chunk).start()
        self.dealt[self.inner, chunk] = self.own[self.inner * self.share + chunk]

    def combine(self, chunk):
        for step in range(1, self.group):
            self.deal_copy(step, chunk).wait_recv()
        order = range(self.group)
        row = pl.ds(self.inner * self.share + chunk, 1)
        passed, through = None, []
        for place in reversed(order) if self.back else order:
            through.append((place, passed))
            factor = self.factors[place, row, :]
            term = self.dealt[place, chunk]
            if passed is None:
                total, passed = term, factor
                self.given[place, chunk] = jnp.zeros_like(term)
            else:
                self.given[place, chunk] = total
                total, passed = total * factor + term, passed * factor
        if self.chain > 1:

            @pl.when(self.first())
            def _():
                self.came[chunk] = jnp.zeros_like(total)

            @pl.when(jnp.logical_not(self.first()))
            def _():
                self.chain_copy(chunk).wait_recv()

            before = self.came[chunk]
            self.gone[chunk] = before * passed + total

            @pl.when(jnp.logical_not(self.last()))
            def _():
                self.chain_copy(chunk).start()

            for place, factor in through:
                added = before if factor is None else before * factor
                self.given[place, chunk] += added
        for step in range(1, self.group):
            self.give_copy(step, chunk).start()
        self.got[self.inner * self.share + chunk] = self.given[self.inner, chunk]

    def arrive(self, chunk):
        for step in range(1, self.group):
            self.give_copy(step, chunk).wait_recv()

    def finish(self):
        for chunk in range(self.share):
            for step in range(1, self.group):
                self.deal_copy(step, chunk).wait_send()
                self.give_copy(step, chunk).wait_send()
            if self.chain > 1:

                @pl.when(jnp.logical_not(self.last()))
                def _():
                    self.chain_copy(chunk).wait_send()


def kernel(
    group, chain, split_heads,
    q_from, k_from, v_from, decay_from, agent_from, gain_from, grad_from,
    y_to, q_grad_to, k_grad_to, v_grad_to, decay_grad_to, gain_grad_to,
    q_ref, k_ref, v_ref, decay_ref, agent_ref, gain_ref, grad_ref,
    y_ref, q_grad_ref, k_grad_ref, v_grad_ref, decay_grad_ref, gain_grad_ref,
    sum_ref, total_ref, spread_ref, bias_ref, factor_ref, score_ref, weight_ref, out_ref, adjoint_ref,
    k_part_ref, v_part_ref, norm_ref, scale_ref, change_ref, gain_ref_in, gain_ref_out,
    end_ref, dealt_ref, came_ref, gone_ref, given_ref, state_ref,
    start_ref, dealt_back_ref, came_back_ref, gone_back_ref, given_back_ref, later_ref,
    load_sems, store_sems, scan_sems, chain_sems, factor_sems, norm_sems, gain_sems_in, gain_sems_out,
):
    loads = [
        pltpu.make_async_copy(source, target, load_sems.at[number])
        for number, (source, target) in enumerate(
            [
                (decay_from, decay_ref),
                (k_from, k_ref),
                (v_from, v_ref),
                (q_from, q_ref),
                (agent_from, agent_ref),
                (gain_from, gain_ref),
                (grad_from, grad_ref),
            ]
        )
    ]
    for load in loads:
        load.start()
    stores = [
        pltpu.make_async_copy(source, target, store_sems.at[number])
        for number, (source, target) in enumerate(
            [
                (y_ref, y_to),
                (q_grad_ref, q_grad_to),
                (k_grad_ref, k_grad_to),
                (v_grad_ref, v_grad_to),
                (decay_grad_ref, decay_grad_to),
                (gain_grad_ref, gain_grad_to),
            ]
        )
    ]
    length, width = q_ref.shape
    heads = width // DK
    share = heads // group
    scale = DK**-0.5
    full_width = width * split_heads
    me, side = lax.axis_index("tm"), lax.axis_index("head")
    inner, outer = lax.rem(me, group), lax.div(me, group)

    inner_peers = [outer * group + lax.rem(inner + step, group) for step in range(1, group)]
    outer_peers = [lax.rem(outer + step, chain) * group + inner for step in range(1, chain)]
    side_peers = [lax.rem(side + step, split_heads) for step in range(1, split_heads)]

    barrier = pltpu.get_barrier_semaphore()
    for peer in inner_peers + outer_peers:
        pl.semaphore_signal(barrier, inc=1, device_id={"tm": peer}, device_id_type=MESH)
    for peer in side_peers:
        pl.semaphore_signal(barrier, inc=1, device_id={"head": peer}, device_id_type=MESH)

    def to_peers(ref, place, peers, axis, sems):
        return [
            pltpu.make_async_remote_copy(
                src_ref=ref.at[place],
                dst_ref=ref.at[place],
                send_sem=sems.at[0, number],
                recv_sem=sems.at[1, number],
                device_id={axis: peer},
                device_id_type=MESH,
            )
            for number, peer in enumerate(peers)
        ]

    forward = Scan(
        False, group, chain, share,
        (end_ref, dealt_ref, came_ref, gone_ref, given_ref, state_ref),
        factor_ref, scan_sems.at[0], chain_sems.at[0],
    )
    backward = Scan(
        True, group, chain, share,
        (start_ref, dealt_back_ref, came_back_ref, gone_back_ref, given_back_ref, later_ref),
        factor_ref, scan_sems.at[1], chain_sems.at[1],
    )

    def columns(head):
        return pl.ds(pl.multiple_of(head * DK, DK), DK)

    def row(head):
        return pl.ds(head, 1)

    def each_head(chunk, work):
        def step(place, carry):
            work(place * share + chunk)
            return carry

        lax.fori_loop(0, group, step, None, unroll=UNROLL)

    rows_at = lax.broadcasted_iota(jnp.int32, (length, length), 0)
    lanes_at = lax.broadcasted_iota(jnp.int32, (length, length), 1)
    loads[0].wait()
    decays = split(decay_ref[...], 3)
    up_to = jnp.where(rows_at <= lanes_at, 1.0, 0.0).astype(BF16)
    sum_ref[...] = product(decays, (up_to,), NN)
    total_ref[...] = product(decays, (jnp.ones((length, DK), BF16),), NN)
    factor_ref[inner] = jnp.exp(total_ref[...])

    def own_end(head):
        across = jnp.broadcast_to(sum_ref[row(head), :], (length, length))
        down = across.T
        spread_ref[head] = down
        tail = jnp.exp(total_ref[row(head), :] - down)
        keys = k_ref[:, columns(head)].astype(F32) * tail
        end_ref[head] = product(split(keys), (v_ref[:, columns(head)],), TN)

    for load in loads[1:3]:
        load.wait()
    each_head(0, own_end)
    pl.semaphore_wait(barrier, len(inner_peers) + len(outer_peers) + len(side_peers))
    factor_copies = to_peers(factor_ref, inner, inner_peers, "tm", factor_sems)
    for copy in factor_copies:
        copy.start()
    forward.deal(0)
    for chunk in range(1, share):
        each_head(chunk, own_end)
        forward.deal(chunk)

    for load in loads[3:]:
        load.wait()
    teams = jnp.broadcast_to(lax.div(agent_ref[...], TEAM).astype(F32), (length, length))
    visible = (rows_at >= lanes_at) & (teams == teams.T)
    bias_ref[...] = jnp.where(visible, 0.0, -1e30)

    def own_out(head):
        across = sum_ref[row(head), :]
        weight = jnp.exp(spread_ref[head] - across + bias_ref[...])
        weight_ref[head] = weight
        score = product((q_ref[:, columns(head)],), (k_ref[:, columns(head)],), NT) * weight * scale
        score_ref[head] = score
        out_ref[head] = product(split(score), (v_ref[:, columns(head)],), NN)

    for copy in factor_copies:
        copy.wait_recv()
    for chunk in range(share):
        forward.combine(chunk)
        each_head(chunk, own_out)

    norm_ref[side] = jnp.zeros_like(norm_ref[side])

    def whole_out(head):
        reached = product((q_ref[:, columns(head)],), split(state_ref[head]), NN)
        out = out_ref[head] + jnp.exp(spread_ref[head]) * scale * reached
        out_ref[head] = out
        gained = grad_ref[:, columns(head)].astype(F32) * gain_ref[row(head), :]
        norm_ref[side, 0] += out * out
        norm_ref[side, 1] += gained * out

    for chunk in range(share):
        forward.arrive(chunk)
        each_head(chunk, whole_out)

    norm_copies = to_peers(norm_ref, side, side_peers, "head", norm_sems)
    for copy in norm_copies:
        copy.start()
    for copy in norm_copies:
        copy.wait_recv()
    squares, inners = norm_ref[0, 0], norm_ref[0, 1]
    for place in range(1, split_heads):
        squares, inners = squares + norm_ref[place, 0], inners + norm_ref[place, 1]
    rms = jnp.sqrt(jnp.sum(squares, axis=1, keepdims=True) / full_width + EPS)
    bent = jnp.sum(inners, axis=1, keepdims=True) / (full_width * rms * rms * rms)
    scale_ref[0] = jnp.broadcast_to(1.0 / rms, (length, DK))
    scale_ref[1] = jnp.broadcast_to(bent, (length, DK))

    def own_start(head):
        gained = grad_ref[:, columns(head)].astype(F32) * gain_ref[row(head), :]
        adjoint = gained * scale_ref[0] - out_ref[head] * scale_ref[1]
        adjoint_ref[head] = adjoint
        weighted = adjoint * jnp.exp(spread_ref[head]) * scale
        start_ref[head] = product((q_ref[:, columns(head)],), split(weighted), TN)

    for chunk in range(share):
        each_head(chunk, own_start)
        backward.deal(chunk)

    def result(head):
        normed = out_ref[head] * scale_ref[0]
        y_ref[:, columns(head)] = (normed * gain_ref[row(head), :]).astype(BF16)
        grads = grad_ref[:, columns(head)].astype(F32)
        gain_ref_in[inner, row(head), :] = jnp.sum(grads * normed, axis=0, keepdims=True)

    for chunk in range(share):
        each_head(chunk, result)
    stores[0].start()
    gain_copies_in = to_peers(gain_ref_in, inner, inner_peers, "tm", gain_sems_in)
    for copy in gain_copies_in:
        copy.start()

    def own_grads(head):
        queries, keys = q_ref[:, columns(head)], k_ref[:, columns(head)]
        adjoint = split(adjoint_ref[head])
        pairs = split(product(adjoint, (v_ref[:, columns(head)],), NT) * weight_ref[head])
        reached = product(adjoint, split(state_ref[head]), NT) * jnp.exp(spread_ref[head])
        q_grad = (product(pairs, (keys,), NN) + reached) * scale
        q_grad_ref[:, columns(head)] = q_grad.astype(BF16)
        k_part_ref[head] = product(pairs, (queries,), TN) * scale
        v_part_ref[head] = product(split(score_ref[head]), adjoint, TN)

    for chunk in range(share):
        backward.combine(chunk)
        each_head(chunk, own_grads)
    stores[1].start()

    for copy in gain_copies_in:
        copy.wait_recv()
    gain_sum = gain_ref_in[0]
    for place in range(1, group):
        gain_sum = gain_sum + gain_ref_in[place]
    gain_ref_out[outer] = gain_sum
    gain_copies_out = to_peers(gain_ref_out, outer, outer_peers, "tm", gain_sems_out)
    for copy in gain_copies_out:
        copy.start()

    ones = jnp.ones((16, DK), BF16)
    ends_here = rows_at == length - 1

    def whole_grads(head):
        later = later_ref[head]
        parts = split(later)
        keys = k_ref[:, columns(head)]
        tail = jnp.exp(total_ref[row(head), :] - spread_ref[head])
        k_grad = k_part_ref[head] + tail * product((v_ref[:, columns(head)],), parts, NT)
        v_grad = v_part_ref[head] + tail * product((keys,), parts, NN)
        k_grad_ref[:, columns(head)] = k_grad.astype(BF16)
        v_grad_ref[:, columns(head)] = v_grad.astype(BF16)
        after = state_ref[head] * jnp.exp(total_ref[row(head), :]) + end_ref[head]
        at_end = jnp.sum(after * later, axis=0, keepdims=True)
        change = out_ref[head] * adjoint_ref[head] - keys.astype(F32) * k_grad
        change = change + jnp.where(ends_here, at_end, 0.0)
        change_ref[row(head), :] = product((ones,), split(change, 3), NT)[:1]

    for chunk in range(share):
        backward.arrive(chunk)
        each_head(chunk, whole_grads)
    stores[2].start()
    stores[3].start()
    from_here = jnp.where(rows_at >= lanes_at, 1.0, 0.0).astype(BF16)
    decay_grad_ref[...] = product(split(change_ref[...], 3), (from_here,), NN)
    stores[4].start()

    for copy in gain_copies_out:
        copy.wait_recv()
    gain_sum = gain_ref_out[0]
    for place in range(1, chain):
        gain_sum = gain_sum + gain_ref_out[place]
    gain_grad_ref[...] = gain_sum
    stores[5].start()

    forward.finish()
    backward.finish()
    for copy in factor_copies + norm_copies + gain_copies_in + gain_copies_out:
        copy.wait_send()
    for store in stores:
        store.wait()


def writer(*refs):
    *arrays, sems = refs
    half = len(arrays) // 2
    copies = [
        pltpu.make_async_copy(source, target, sems.at[number])
        for number, (source, target) in enumerate(zip(arrays[:half], arrays[half:]))
    ]
    for copy in copies:
        copy.start()
    for copy in copies:
        copy.wait()


def body(group, chain, split_heads, queries, keys, values, log_decay, agent_ids, norm_gain, out_grad):
    length, width = queries.shape
    heads = width // DK
    share = heads // group
    state = (DK, DK)
    row_shape = (heads, DK)
    travelling = [
        pltpu.VMEM((heads, *state), F32),
        pltpu.VMEM((group, share, *state), F32),
        pltpu.VMEM((share, *state), F32),
        pltpu.VMEM((share, *state), F32),
        pltpu.VMEM((group, share, *state), F32),
        pltpu.VMEM((heads, *state), F32),
    ]
    per_head = pltpu.VMEM((heads, length, DK), F32)
    peers, others, sides = max(1, group - 1), max(1, chain - 1), max(1, split_heads - 1)
    wide = jax.ShapeDtypeStruct((length, width), BF16)
    outs = pl.pallas_call(
        functools.partial(kernel, group, chain, split_heads),
        out_shape=[
            wide,
            wide,
            wide,
            wide,
            jax.ShapeDtypeStruct((heads, length), F32),
            jax.ShapeDtypeStruct((heads, DK), F32),
        ],
        in_specs=[pl.BlockSpec(memory_space=pltpu.HBM)] * 7,
        out_specs=[pl.BlockSpec(memory_space=pltpu.HBM)] * 6,
        scratch_shapes=[
            *[pltpu.VMEM((length, width), BF16)] * 3,
            pltpu.VMEM((heads, length), F32),
            pltpu.VMEM((1, length), agent_ids.dtype),
            pltpu.VMEM(row_shape, F32),
            pltpu.VMEM((length, width), BF16),
            *[pltpu.VMEM((length, width), BF16)] * 4,
            pltpu.VMEM((heads, length), F32),
            pltpu.VMEM(row_shape, F32),
            pltpu.VMEM(row_shape, F32),
            pltpu.VMEM(row_shape, F32),
            per_head,
            pltpu.VMEM((length, length), F32),
            pltpu.VMEM((group, *row_shape), F32),
            per_head,
            per_head,
            per_head,
            per_head,
            per_head,
            per_head,
            pltpu.VMEM((split_heads, 2, length, DK), F32),
            pltpu.VMEM((2, length, DK), F32),
            pltpu.VMEM(row_shape, F32),
            pltpu.VMEM((group, *row_shape), F32),
            pltpu.VMEM((chain, *row_shape), F32),
            *travelling,
            *travelling,
            pltpu.SemaphoreType.DMA((7,)),
            pltpu.SemaphoreType.DMA((6,)),
            pltpu.SemaphoreType.DMA((2, 2, 2, peers, share)),
            pltpu.SemaphoreType.DMA((2, 2, share)),
            pltpu.SemaphoreType.DMA((2, peers)),
            pltpu.SemaphoreType.DMA((2, sides)),
            pltpu.SemaphoreType.DMA((2, peers)),
            pltpu.SemaphoreType.DMA((2, others)),
        ],
        compiler_params=pltpu.CompilerParams(
            collective_id=0, has_side_effects=True, vmem_limit_bytes=60 * 2**20
        ),
        cost_estimate=pl.CostEstimate(
            flops=heads * 28 * 2 * DK**3,
            bytes_accessed=8 * length * width * 2,
            transcendentals=heads * 5 * DK**2,
        ),
    )(
        queries,
        keys,
        values,
        log_decay,
        agent_ids.reshape(1, length),
        norm_gain.reshape(heads, DK),
        out_grad,
    )
    outs = pl.pallas_call(
        writer,
        out_shape=[jax.ShapeDtypeStruct(out.shape, out.dtype) for out in outs],
        in_specs=[pl.BlockSpec(memory_space=pltpu.HBM)] * 6,
        out_specs=[pl.BlockSpec(memory_space=pltpu.HBM)] * 6,
        scratch_shapes=[pltpu.SemaphoreType.DMA((6,))],
        compiler_params=pltpu.CompilerParams(vmem_limit_bytes=60 * 2**20),
    )(*outs)
    return (*outs[:5], outs[5].reshape(width))


def solution(mesh):
    count, split_heads = mesh.shape["tm"], mesh.shape["head"]

    def placed_body(queries, *rest):
        group = math.gcd(math.gcd(count, queries.shape[1] // DK), 4)
        return body(group, count // group, split_heads, queries, *rest)

    wide = P("tm", "head")
    return jax.shard_map(
        placed_body,
        mesh=mesh,
        in_specs=(wide, wide, wide, P("head", "tm"), P("tm"), P("head"), wide),
        out_specs=(wide, wide, wide, wide, P("head", "tm"), P("head")),
        check_vma=False,
    )
```

```python
import functools
import math

import jax
import jax.numpy as jnp
from jax import lax
from jax.experimental import pallas as pl
from jax.experimental.pallas import tpu as pltpu
from jax.sharding import PartitionSpec as P

DK = 128
TEAM = 16
EPS = 1e-06
UNROLL = 4
MESH = pl.DeviceIdType.MESH
F32, BF16 = jnp.float32, jnp.bfloat16
NN, NT, TN = ((1,), (0,)), ((1,), (1,)), ((0,), (0,))


def split(value, count=2):
    parts = []
    for _ in range(count):
        part = value.astype(BF16)
        parts.append(part)
        value = value - part.astype(F32)
    return tuple(parts)


def product(left, right, form):
    order = max(len(left), len(right))
    pairs = [(a, b) for i, a in enumerate(left) for j, b in enumerate(right) if i + j < order]
    lefts = jnp.concatenate([a for a, _ in pairs], axis=form[0][0])
    rights = jnp.concatenate([b for _, b in pairs], axis=form[1][0])
    return lax.dot_general(lefts, rights, (form, ((), ())), preferred_element_type=F32)


class Scan:
    def __init__(self, back, group, chain, share, refs, factors, sems, chain_sems):
        self.back, self.group, self.chain, self.share = back, group, chain, share
        self.own, self.dealt, self.came, self.gone, self.given, self.got = refs
        self.factors, self.sems, self.chain_sems = factors, sems, chain_sems
        me = lax.axis_index("tm")
        self.inner, self.outer = lax.rem(me, group), lax.div(me, group)
        self.sent = []

    def peer(self, step):
        return lax.rem(self.inner + step, self.group)

    def copy(self, source, target, send, receive, outer, inner):
        return pltpu.make_async_remote_copy(
            src_ref=source,
            dst_ref=target,
            send_sem=send,
            recv_sem=receive,
            device_id={"tm": outer * self.group + inner},
            device_id_type=MESH,
        )

    def deal_copy(self, step, chunk):
        peer = self.peer(step)
        sems = self.sems.at[0, :, step - 1, chunk]
        return self.copy(
            self.own.at[peer * self.share + chunk],
            self.dealt.at[self.inner, chunk],
            sems.at[0],
            sems.at[1],
            self.outer,
            peer,
        )

    def give_copy(self, step, chunk):
        peer = self.peer(step)
        sems = self.sems.at[1, :, step - 1, chunk]
        return self.copy(
            self.given.at[peer, chunk],
            self.got.at[self.inner * self.share + chunk],
            sems.at[0],
            sems.at[1],
            self.outer,
            peer,
        )

    def chain_copy(self, chunk):
        outer = self.outer + (-1 if self.back else 1)
        outer = lax.rem(outer + self.chain, self.chain)
        sems = self.chain_sems
        return self.copy(
            self.gone.at[chunk],
            self.came.at[chunk],
            sems.at[0, chunk],
            sems.at[1, chunk],
            outer,
            self.inner,
        )

    def first(self):
        return self.outer == (self.chain - 1 if self.back else 0)

    def last(self):
        return self.outer == (0 if self.back else self.chain - 1)

    def deal(self, chunk):
        for step in range(1, self.group):
            self.deal_copy(step, chunk).start()
        self.dealt[self.inner, chunk] = self.own[self.inner * self.share + chunk]

    def combine(self, chunk):
        for step in range(1, self.group):
            self.deal_copy(step, chunk).wait_recv()
        order = range(self.group)
        row = pl.ds(self.inner * self.share + chunk, 1)
        passed, through = None, []
        for place in reversed(order) if self.back else order:
            through.append((place, passed))
            factor = self.factors[place, row, :]
            term = self.dealt[place, chunk]
            if passed is None:
                total, passed = term, factor
                self.given[place, chunk] = jnp.zeros_like(term)
            else:
                self.given[place, chunk] = total
                total, passed = total * factor + term, passed * factor
        if self.chain > 1:

            @pl.when(self.first())
            def _():
                self.came[chunk] = jnp.zeros_like(total)

            @pl.when(jnp.logical_not(self.first()))
            def _():
                self.chain_copy(chunk).wait_recv()

            before = self.came[chunk]
            self.gone[chunk] = before * passed + total

            @pl.when(jnp.logical_not(self.last()))
            def _():
                self.chain_copy(chunk).start()

            for place, factor in through:
                added = before if factor is None else before * factor
                self.given[place, chunk] += added
        for step in range(1, self.group):
            self.give_copy(step, chunk).start()
        self.got[self.inner * self.share + chunk] = self.given[self.inner, chunk]

    def arrive(self, chunk):
        for step in range(1, self.group):
            self.give_copy(step, chunk).wait_recv()

    def finish(self):
        for chunk in range(self.share):
            for step in range(1, self.group):
                self.deal_copy(step, chunk).wait_send()
                self.give_copy(step, chunk).wait_send()
            if self.chain > 1:

                @pl.when(jnp.logical_not(self.last()))
                def _():
                    self.chain_copy(chunk).wait_send()


def kernel(
    group, chain, split_heads,
    q_from, k_from, v_from, decay_from, agent_from, gain_from, grad_from,
    y_to, q_grad_to, k_grad_to, v_grad_to, decay_grad_to, gain_grad_to,
    q_ref, k_ref, v_ref, decay_ref, agent_ref, gain_ref, grad_ref,
    y_ref, q_grad_ref, k_grad_ref, v_grad_ref, decay_grad_ref, gain_grad_ref,
    sum_ref, total_ref, spread_ref, bias_ref, factor_ref, score_ref, weight_ref, out_ref, adjoint_ref,
    k_part_ref, v_part_ref, norm_ref, scale_ref, change_ref, gain_ref_in, gain_ref_out,
    end_ref, dealt_ref, came_ref, gone_ref, given_ref, state_ref,
    start_ref, dealt_back_ref, came_back_ref, gone_back_ref, given_back_ref, later_ref,
    load_sems, store_sems, scan_sems, chain_sems, factor_sems, norm_sems, gain_sems_in, gain_sems_out,
):
    loads = [
        pltpu.make_async_copy(source, target, load_sems.at[number])
        for number, (source, target) in enumerate(
            [
                (decay_from, decay_ref),
                (k_from, k_ref),
                (v_from, v_ref),
                (q_from, q_ref),
                (agent_from, agent_ref),
                (gain_from, gain_ref),
                (grad_from, grad_ref),
            ]
        )
    ]
    for load in loads:
        load.start()
    stores = [
        pltpu.make_async_copy(source, target, store_sems.at[number])
        for number, (source, target) in enumerate(
            [
                (y_ref, y_to),
                (q_grad_ref, q_grad_to),
                (k_grad_ref, k_grad_to),
                (v_grad_ref, v_grad_to),
                (decay_grad_ref, decay_grad_to),
                (gain_grad_ref, gain_grad_to),
            ]
        )
    ]
    length, width = q_ref.shape
    heads = width // DK
    share = heads // group
    scale = DK**-0.5
    full_width = width * split_heads
    me, side = lax.axis_index("tm"), lax.axis_index("head")
    inner, outer = lax.rem(me, group), lax.div(me, group)

    inner_peers = [outer * group + lax.rem(inner + step, group) for step in range(1, group)]
    outer_peers = [lax.rem(outer + step, chain) * group + inner for step in range(1, chain)]
    side_peers = [lax.rem(side + step, split_heads) for step in range(1, split_heads)]

    barrier = pltpu.get_barrier_semaphore()
    for peer in inner_peers + outer_peers:
        pl.semaphore_signal(barrier, inc=1, device_id={"tm": peer}, device_id_type=MESH)
    for peer in side_peers:
        pl.semaphore_signal(barrier, inc=1, device_id={"head": peer}, device_id_type=MESH)

    def to_peers(ref, place, peers, axis, sems):
        return [
            pltpu.make_async_remote_copy(
                src_ref=ref.at[place],
                dst_ref=ref.at[place],
                send_sem=sems.at[0, number],
                recv_sem=sems.at[1, number],
                device_id={axis: peer},
                device_id_type=MESH,
            )
            for number, peer in enumerate(peers)
        ]

    forward = Scan(
        False, group, chain, share,
        (end_ref, dealt_ref, came_ref, gone_ref, given_ref, state_ref),
        factor_ref, scan_sems.at[0], chain_sems.at[0],
    )
    backward = Scan(
        True, group, chain, share,
        (start_ref, dealt_back_ref, came_back_ref, gone_back_ref, given_back_ref, later_ref),
        factor_ref, scan_sems.at[1], chain_sems.at[1],
    )

    def columns(head):
        return pl.ds(pl.multiple_of(head * DK, DK), DK)

    def row(head):
        return pl.ds(head, 1)

    def each_head(chunk, work):
        def step(place, carry):
            work(place * share + chunk)
            return carry

        lax.fori_loop(0, group, step, None, unroll=UNROLL)

    rows_at = lax.broadcasted_iota(jnp.int32, (length, length), 0)
    lanes_at = lax.broadcasted_iota(jnp.int32, (length, length), 1)
    loads[0].wait()
    decays = split(decay_ref[...], 3)
    up_to = jnp.where(rows_at <= lanes_at, 1.0, 0.0).astype(BF16)
    sum_ref[...] = product(decays, (up_to,), NN)
    total_ref[...] = product(decays, (jnp.ones((length, DK), BF16),), NN)
    factor_ref[inner] = jnp.exp(total_ref[...])

    def own_end(head):
        across = jnp.broadcast_to(sum_ref[row(head), :], (length, length))
        down = across.T
        spread_ref[head] = down
        tail = jnp.exp(total_ref[row(head), :] - down)
        keys = k_ref[:, columns(head)].astype(F32) * tail
        end_ref[head] = product(split(keys), (v_ref[:, columns(head)],), TN)

    for load in loads[1:3]:
        load.wait()
    each_head(0, own_end)
    pl.semaphore_wait(barrier, len(inner_peers) + len(outer_peers) + len(side_peers))
    factor_copies = to_peers(factor_ref, inner, inner_peers, "tm", factor_sems)
    for copy in factor_copies:
        copy.start()
    forward.deal(0)
    for chunk in range(1, share):
        each_head(chunk, own_end)
        forward.deal(chunk)

    for load in loads[3:]:
        load.wait()
    teams = jnp.broadcast_to(lax.div(agent_ref[...], TEAM).astype(F32), (length, length))
    visible = (rows_at >= lanes_at) & (teams == teams.T)
    bias_ref[...] = jnp.where(visible, 0.0, -1e30)

    def own_out(head):
        across = sum_ref[row(head), :]
        weight = jnp.exp(spread_ref[head] - across + bias_ref[...])
        weight_ref[head] = weight
        score = product((q_ref[:, columns(head)],), (k_ref[:, columns(head)],), NT) * weight * scale
        score_ref[head] = score
        out_ref[head] = product(split(score), (v_ref[:, columns(head)],), NN)

    for copy in factor_copies:
        copy.wait_recv()
    for chunk in range(share):
        forward.combine(chunk)
        each_head(chunk, own_out)

    norm_ref[side] = jnp.zeros_like(norm_ref[side])

    def whole_out(head):
        reached = product((q_ref[:, columns(head)],), split(state_ref[head]), NN)
        out = out_ref[head] + jnp.exp(spread_ref[head]) * scale * reached
        out_ref[head] = out
        gained = grad_ref[:, columns(head)].astype(F32) * gain_ref[row(head), :]
        norm_ref[side, 0] += out * out
        norm_ref[side, 1] += gained * out

    for chunk in range(share):
        forward.arrive(chunk)
        each_head(chunk, whole_out)

    norm_copies = to_peers(norm_ref, side, side_peers, "head", norm_sems)
    for copy in norm_copies:
        copy.start()
    for copy in norm_copies:
        copy.wait_recv()
    squares, inners = norm_ref[0, 0], norm_ref[0, 1]
    for place in range(1, split_heads):
        squares, inners = squares + norm_ref[place, 0], inners + norm_ref[place, 1]
    rms = jnp.sqrt(jnp.sum(squares, axis=1, keepdims=True) / full_width + EPS)
    bent = jnp.sum(inners, axis=1, keepdims=True) / (full_width * rms * rms * rms)
    scale_ref[0] = jnp.broadcast_to(1.0 / rms, (length, DK))
    scale_ref[1] = jnp.broadcast_to(bent, (length, DK))

    def own_start(head):
        gained = grad_ref[:, columns(head)].astype(F32) * gain_ref[row(head), :]
        adjoint = gained * scale_ref[0] - out_ref[head] * scale_ref[1]
        adjoint_ref[head] = adjoint
        weighted = adjoint * jnp.exp(spread_ref[head]) * scale
        start_ref[head] = product((q_ref[:, columns(head)],), split(weighted), TN)

    for chunk in range(share):
        each_head(chunk, own_start)
        backward.deal(chunk)

    def result(head):
        normed = out_ref[head] * scale_ref[0]
        y_ref[:, columns(head)] = (normed * gain_ref[row(head), :]).astype(BF16)
        grads = grad_ref[:, columns(head)].astype(F32)
        gain_ref_in[inner, row(head), :] = jnp.sum(grads * normed, axis=0, keepdims=True)

    for chunk in range(share):
        each_head(chunk, result)
    stores[0].start()
    gain_copies_in = to_peers(gain_ref_in, inner, inner_peers, "tm", gain_sems_in)
    for copy in gain_copies_in:
        copy.start()

    def own_grads(head):
        queries, keys = q_ref[:, columns(head)], k_ref[:, columns(head)]
        adjoint = split(adjoint_ref[head])
        pairs = split(product(adjoint, (v_ref[:, columns(head)],), NT) * weight_ref[head])
        reached = product(adjoint, split(state_ref[head]), NT) * jnp.exp(spread_ref[head])
        q_grad = (product(pairs, (keys,), NN) + reached) * scale
        q_grad_ref[:, columns(head)] = q_grad.astype(BF16)
        k_part_ref[head] = product(pairs, (queries,), TN) * scale
        v_part_ref[head] = product(split(score_ref[head]), adjoint, TN)

    for chunk in range(share):
        backward.combine(chunk)
        each_head(chunk, own_grads)
    stores[1].start()

    for copy in gain_copies_in:
        copy.wait_recv()
    gain_sum = gain_ref_in[0]
    for place in range(1, group):
        gain_sum = gain_sum + gain_ref_in[place]
    gain_ref_out[outer] = gain_sum
    gain_copies_out = to_peers(gain_ref_out, outer, outer_peers, "tm", gain_sems_out)
    for copy in gain_copies_out:
        copy.start()

    ones = jnp.ones((16, DK), BF16)
    ends_here = rows_at == length - 1

    def whole_grads(head):
        later = later_ref[head]
        parts = split(later)
        keys = k_ref[:, columns(head)]
        tail = jnp.exp(total_ref[row(head), :] - spread_ref[head])
        k_grad = k_part_ref[head] + tail * product((v_ref[:, columns(head)],), parts, NT)
        v_grad = v_part_ref[head] + tail * product((keys,), parts, NN)
        k_grad_ref[:, columns(head)] = k_grad.astype(BF16)
        v_grad_ref[:, columns(head)] = v_grad.astype(BF16)
        after = state_ref[head] * jnp.exp(total_ref[row(head), :]) + end_ref[head]
        at_end = jnp.sum(after * later, axis=0, keepdims=True)
        change = out_ref[head] * adjoint_ref[head] - keys.astype(F32) * k_grad
        change = change + jnp.where(ends_here, at_end, 0.0)
        change_ref[row(head), :] = product((ones,), split(change, 3), NT)[:1]

    for chunk in range(share):
        backward.arrive(chunk)
        each_head(chunk, whole_grads)
    stores[2].start()
    stores[3].start()
    from_here = jnp.where(rows_at >= lanes_at, 1.0, 0.0).astype(BF16)
    decay_grad_ref[...] = product(split(change_ref[...], 3), (from_here,), NN)
    stores[4].start()

    for copy in gain_copies_out:
        copy.wait_recv()
    gain_sum = gain_ref_out[0]
    for place in range(1, chain):
        gain_sum = gain_sum + gain_ref_out[place]
    gain_grad_ref[...] = gain_sum
    stores[5].start()

    forward.finish()
    backward.finish()
    for copy in factor_copies + norm_copies + gain_copies_in + gain_copies_out:
        copy.wait_send()
    for store in stores:
        store.wait()


def writer(count, *refs):
    sources, targets, between, sems = refs[:count], refs[count : 2 * count], refs[2 * count : -1], refs[-1]
    steps = [
        (
            pltpu.make_async_copy(sources[number], between[number], sems.at[0, number]),
            pltpu.make_async_copy(between[number], targets[number], sems.at[1, number]),
        )
        for number in range(count)
    ]
    for load, _ in steps:
        load.start()
    for load, store in steps:
        load.wait()
        store.start()
    for _, store in steps:
        store.wait()


def body(group, chain, split_heads, queries, keys, values, log_decay, agent_ids, norm_gain, out_grad):
    length, width = queries.shape
    heads = width // DK
    share = heads // group
    state = (DK, DK)
    row_shape = (heads, DK)
    travelling = [
        pltpu.VMEM((heads, *state), F32),
        pltpu.VMEM((group, share, *state), F32),
        pltpu.VMEM((share, *state), F32),
        pltpu.VMEM((share, *state), F32),
        pltpu.VMEM((group, share, *state), F32),
        pltpu.VMEM((heads, *state), F32),
    ]
    per_head = pltpu.VMEM((heads, length, DK), F32)
    peers, others, sides = max(1, group - 1), max(1, chain - 1), max(1, split_heads - 1)
    wide = jax.ShapeDtypeStruct((length, width), BF16)
    outs = pl.pallas_call(
        functools.partial(kernel, group, chain, split_heads),
        out_shape=[
            wide,
            wide,
            wide,
            wide,
            jax.ShapeDtypeStruct((heads, length), F32),
            jax.ShapeDtypeStruct((heads, DK), F32),
        ],
        in_specs=[pl.BlockSpec(memory_space=pltpu.HBM)] * 7,
        out_specs=[pl.BlockSpec(memory_space=pltpu.HBM)] * 6,
        scratch_shapes=[
            *[pltpu.VMEM((length, width), BF16)] * 3,
            pltpu.VMEM((heads, length), F32),
            pltpu.VMEM((1, length), agent_ids.dtype),
            pltpu.VMEM(row_shape, F32),
            pltpu.VMEM((length, width), BF16),
            *[pltpu.VMEM((length, width), BF16)] * 4,
            pltpu.VMEM((heads, length), F32),
            pltpu.VMEM(row_shape, F32),
            pltpu.VMEM(row_shape, F32),
            pltpu.VMEM(row_shape, F32),
            per_head,
            pltpu.VMEM((length, length), F32),
            pltpu.VMEM((group, *row_shape), F32),
            per_head,
            per_head,
            per_head,
            per_head,
            per_head,
            per_head,
            pltpu.VMEM((split_heads, 2, length, DK), F32),
            pltpu.VMEM((2, length, DK), F32),
            pltpu.VMEM(row_shape, F32),
            pltpu.VMEM((group, *row_shape), F32),
            pltpu.VMEM((chain, *row_shape), F32),
            *travelling,
            *travelling,
            pltpu.SemaphoreType.DMA((7,)),
            pltpu.SemaphoreType.DMA((6,)),
            pltpu.SemaphoreType.DMA((2, 2, 2, peers, share)),
            pltpu.SemaphoreType.DMA((2, 2, share)),
            pltpu.SemaphoreType.DMA((2, peers)),
            pltpu.SemaphoreType.DMA((2, sides)),
            pltpu.SemaphoreType.DMA((2, peers)),
            pltpu.SemaphoreType.DMA((2, others)),
        ],
        compiler_params=pltpu.CompilerParams(
            collective_id=0, has_side_effects=True, vmem_limit_bytes=60 * 2**20
        ),
        cost_estimate=pl.CostEstimate(
            flops=heads * 28 * 2 * DK**3,
            bytes_accessed=8 * length * width * 2,
            transcendentals=heads * 5 * DK**2,
        ),
    )(
        queries,
        keys,
        values,
        log_decay,
        agent_ids.reshape(1, length),
        norm_gain.reshape(heads, DK),
        out_grad,
    )
    outs = pl.pallas_call(
        functools.partial(writer, len(outs)),
        out_shape=[jax.ShapeDtypeStruct(out.shape, out.dtype) for out in outs],
        in_specs=[pl.BlockSpec(memory_space=pltpu.HBM)] * 6,
        out_specs=[pl.BlockSpec(memory_space=pltpu.HBM)] * 6,
        scratch_shapes=[pltpu.VMEM(out.shape, out.dtype) for out in outs]
        + [pltpu.SemaphoreType.DMA((2, len(outs)))],
        compiler_params=pltpu.CompilerParams(vmem_limit_bytes=60 * 2**20),
    )(*outs)
    return (*outs[:5], outs[5].reshape(width))


def solution(mesh):
    count, split_heads = mesh.shape["tm"], mesh.shape["head"]

    def placed_body(queries, *rest):
        group = math.gcd(math.gcd(count, queries.shape[1] // DK), 4)
        return body(group, count // group, split_heads, queries, *rest)

    wide = P("tm", "head")
    return jax.shard_map(
        placed_body,
        mesh=mesh,
        in_specs=(wide, wide, wide, P("head", "tm"), P("tm"), P("head"), wide),
        out_specs=(wide, wide, wide, wide, P("head", "tm"), P("head")),
        check_vma=False,
    )
```

```python
import functools
import math

import jax
import jax.numpy as jnp
from jax import lax
from jax.experimental import pallas as pl
from jax.experimental.pallas import tpu as pltpu
from jax.sharding import PartitionSpec as P

DK = 128
TEAM = 16
EPS = 1e-06
UNROLL = 4
MESH = pl.DeviceIdType.MESH
F32, BF16 = jnp.float32, jnp.bfloat16
NN, NT, TN = ((1,), (0,)), ((1,), (1,)), ((0,), (0,))


def split(value, count=2):
    parts = []
    for _ in range(count):
        part = value.astype(BF16)
        parts.append(part)
        value = value - part.astype(F32)
    return tuple(parts)


def product(left, right, form):
    order = max(len(left), len(right))
    pairs = [(a, b) for i, a in enumerate(left) for j, b in enumerate(right) if i + j < order]
    lefts = jnp.concatenate([a for a, _ in pairs], axis=form[0][0])
    rights = jnp.concatenate([b for _, b in pairs], axis=form[1][0])
    return lax.dot_general(lefts, rights, (form, ((), ())), preferred_element_type=F32)


class Scan:
    def __init__(self, back, group, chain, share, refs, factors, sems, chain_sems):
        self.back, self.group, self.chain, self.share = back, group, chain, share
        self.own, self.dealt, self.came, self.gone, self.given, self.got = refs
        self.factors, self.sems, self.chain_sems = factors, sems, chain_sems
        me = lax.axis_index("tm")
        self.inner, self.outer = lax.rem(me, group), lax.div(me, group)
        self.sent = []

    def peer(self, step):
        return lax.rem(self.inner + step, self.group)

    def copy(self, source, target, send, receive, outer, inner):
        return pltpu.make_async_remote_copy(
            src_ref=source,
            dst_ref=target,
            send_sem=send,
            recv_sem=receive,
            device_id={"tm": outer * self.group + inner},
            device_id_type=MESH,
        )

    def deal_copy(self, step, chunk):
        peer = self.peer(step)
        sems = self.sems.at[0, :, step - 1, chunk]
        return self.copy(
            self.own.at[peer * self.share + chunk],
            self.dealt.at[self.inner, chunk],
            sems.at[0],
            sems.at[1],
            self.outer,
            peer,
        )

    def give_copy(self, step, chunk):
        peer = self.peer(step)
        sems = self.sems.at[1, :, step - 1, chunk]
        return self.copy(
            self.given.at[peer, chunk],
            self.got.at[self.inner * self.share + chunk],
            sems.at[0],
            sems.at[1],
            self.outer,
            peer,
        )

    def chain_copy(self, chunk):
        outer = self.outer + (-1 if self.back else 1)
        outer = lax.rem(outer + self.chain, self.chain)
        sems = self.chain_sems
        return self.copy(
            self.gone.at[chunk],
            self.came.at[chunk],
            sems.at[0, chunk],
            sems.at[1, chunk],
            outer,
            self.inner,
        )

    def first(self):
        return self.outer == (self.chain - 1 if self.back else 0)

    def last(self):
        return self.outer == (0 if self.back else self.chain - 1)

    def deal(self, chunk):
        for step in range(1, self.group):
            if chunk > 0:
                self.deal_copy(step, chunk - 1).wait_send()
            self.deal_copy(step, chunk).start()
        self.dealt[self.inner, chunk] = self.own[self.inner * self.share + chunk]

    def total(self, chunk):
        for step in range(1, self.group):
            self.deal_copy(step, chunk).wait_recv()
        order = range(self.group)
        row = pl.ds(self.inner * self.share + chunk, 1)
        passed = None
        for place in reversed(order) if self.back else order:
            factor = self.factors[place, row, :]
            term = self.dealt[place, chunk]
            if passed is None:
                total, passed = term, factor
                self.given[place, chunk] = jnp.zeros_like(term)
            else:
                self.given[place, chunk] = total
                total, passed = total * factor + term, passed * factor
        self.gone[chunk] = total

    def link(self, chunk):
        order = range(self.group)
        row = pl.ds(self.inner * self.share + chunk, 1)
        passed, through = None, []
        for place in reversed(order) if self.back else order:
            through.append((place, passed))
            factor = self.factors[place, row, :]
            passed = factor if passed is None else passed * factor

        @pl.when(jnp.logical_not(self.first()))
        def _():
            self.chain_copy(chunk).wait_recv()
            self.gone[chunk] += self.came[chunk] * passed

        @pl.when(jnp.logical_not(self.last()))
        def _():
            self.chain_copy(chunk).start()

        @pl.when(jnp.logical_not(self.first()))
        def _():
            before = self.came[chunk]
            for place, factor in through:
                added = before if factor is None else before * factor
                self.given[place, chunk] += added

    def run(self, make, between):
        share, last = self.share, self.share - 1
        distance = self.chain - 1 - self.outer if self.back else self.outer
        for chunk in range(min(2, share)):
            make(chunk)
            self.deal(chunk)
        for chunk in range(2, share):
            make(chunk)
        early = share - 2
        for slot in range(early):
            self.total(slot)
            if self.chain > 1:
                for chunk in range(slot + 1):

                    @pl.when(distance == slot - chunk)
                    def _():
                        self.link(chunk)

            self.deal(slot + 2)
        for step in range(1, self.group):
            self.deal_copy(step, last).wait_send()
        for chunk in range(share):
            if chunk >= early:
                self.total(chunk)
            if self.chain > 1:

                @pl.when(distance > early - 1 - chunk)
                def _():
                    self.link(chunk)

            self.give(chunk)
            between(chunk)

    def give(self, chunk):
        for step in range(1, self.group):
            self.give_copy(step, chunk).start()
        self.got[self.inner * self.share + chunk] = self.given[self.inner, chunk]

    def arrive(self, chunk):
        for step in range(1, self.group):
            self.give_copy(step, chunk).wait_recv()

    def finish(self):
        for chunk in range(self.share):
            for step in range(1, self.group):
                self.give_copy(step, chunk).wait_send()
            if self.chain > 1:

                @pl.when(jnp.logical_not(self.last()))
                def _():
                    self.chain_copy(chunk).wait_send()


def kernel(
    group, chain, split_heads,
    q_from, k_from, v_from, decay_from, agent_from, gain_from, grad_from,
    y_to, q_grad_to, k_grad_to, v_grad_to, decay_grad_to, gain_grad_to,
    q_ref, k_ref, v_ref, decay_ref, agent_ref, gain_ref, grad_ref,
    y_ref, q_grad_ref, k_grad_ref, v_grad_ref, decay_grad_ref, gain_grad_ref,
    sum_ref, total_ref, spread_ref, bias_ref, factor_ref, score_ref, weight_ref, out_ref, adjoint_ref,
    k_part_ref, v_part_ref, norm_ref, scale_ref, change_ref, gain_ref_in, gain_ref_out,
    end_ref, dealt_ref, came_ref, gone_ref, given_ref, state_ref,
    start_ref, dealt_back_ref, came_back_ref, gone_back_ref, given_back_ref, later_ref,
    load_sems, store_sems, scan_sems, chain_sems, factor_sems, norm_sems, gain_sems_in, gain_sems_out,
):
    loads = [
        pltpu.make_async_copy(source, target, load_sems.at[number])
        for number, (source, target) in enumerate(
            [
                (decay_from, decay_ref),
                (k_from, k_ref),
                (v_from, v_ref),
                (q_from, q_ref),
                (agent_from, agent_ref),
                (gain_from, gain_ref),
                (grad_from, grad_ref),
            ]
        )
    ]
    for load in loads:
        load.start()
    stores = [
        pltpu.make_async_copy(source, target, store_sems.at[number])
        for number, (source, target) in enumerate(
            [
                (y_ref, y_to),
                (q_grad_ref, q_grad_to),
                (k_grad_ref, k_grad_to),
                (v_grad_ref, v_grad_to),
                (decay_grad_ref, decay_grad_to),
                (gain_grad_ref, gain_grad_to),
            ]
        )
    ]
    length, width = q_ref.shape
    heads = width // DK
    share = heads // group
    scale = DK**-0.5
    full_width = width * split_heads
    me, side = lax.axis_index("tm"), lax.axis_index("head")
    inner, outer = lax.rem(me, group), lax.div(me, group)

    inner_peers = [outer * group + lax.rem(inner + step, group) for step in range(1, group)]
    outer_peers = [lax.rem(outer + step, chain) * group + inner for step in range(1, chain)]
    side_peers = [lax.rem(side + step, split_heads) for step in range(1, split_heads)]

    barrier = pltpu.get_barrier_semaphore()
    for peer in inner_peers + outer_peers:
        pl.semaphore_signal(barrier, inc=1, device_id={"tm": peer}, device_id_type=MESH)
    for peer in side_peers:
        pl.semaphore_signal(barrier, inc=1, device_id={"head": peer}, device_id_type=MESH)

    def to_peers(ref, place, peers, axis, sems):
        return [
            pltpu.make_async_remote_copy(
                src_ref=ref.at[place],
                dst_ref=ref.at[place],
                send_sem=sems.at[0, number],
                recv_sem=sems.at[1, number],
                device_id={axis: peer},
                device_id_type=MESH,
            )
            for number, peer in enumerate(peers)
        ]

    forward = Scan(
        False, group, chain, share,
        (end_ref, dealt_ref, came_ref, gone_ref, given_ref, state_ref),
        factor_ref, scan_sems.at[0], chain_sems.at[0],
    )
    backward = Scan(
        True, group, chain, share,
        (start_ref, dealt_back_ref, came_back_ref, gone_back_ref, given_back_ref, later_ref),
        factor_ref, scan_sems.at[1], chain_sems.at[1],
    )

    def columns(head):
        return pl.ds(pl.multiple_of(head * DK, DK), DK)

    def row(head):
        return pl.ds(head, 1)

    def each_head(chunk, work):
        def step(place, carry):
            work(place * share + chunk)
            return carry

        lax.fori_loop(0, group, step, None, unroll=UNROLL)

    rows_at = lax.broadcasted_iota(jnp.int32, (length, length), 0)
    lanes_at = lax.broadcasted_iota(jnp.int32, (length, length), 1)
    loads[0].wait()
    decays = split(decay_ref[...], 3)
    up_to = jnp.where(rows_at <= lanes_at, 1.0, 0.0).astype(BF16)
    sum_ref[...] = product(decays, (up_to,), NN)
    total_ref[...] = product(decays, (jnp.ones((length, DK), BF16),), NN)
    factor_ref[inner] = jnp.exp(total_ref[...])

    def own_end(head):
        across = jnp.broadcast_to(sum_ref[row(head), :], (length, length))
        down = across.T
        spread_ref[head] = down
        tail = jnp.exp(total_ref[row(head), :] - down)
        keys = k_ref[:, columns(head)].astype(F32) * tail
        end_ref[head] = product(split(keys), (v_ref[:, columns(head)],), TN)

    for load in loads[1:3]:
        load.wait()
    factor_copies = to_peers(factor_ref, inner, inner_peers, "tm", factor_sems)

    def make_ends(chunk):
        each_head(chunk, own_end)
        if chunk == 0:
            pl.semaphore_wait(barrier, len(inner_peers) + len(outer_peers) + len(side_peers))
            for copy in factor_copies:
                copy.start()
        if chunk == share - 1:
            for load in loads[3:]:
                load.wait()
            make_bias()
            for copy in factor_copies:
                copy.wait_recv()

    def make_bias():
        teams = jnp.broadcast_to(lax.div(agent_ref[...], TEAM).astype(F32), (length, length))
        visible = (rows_at >= lanes_at) & (teams == teams.T)
        bias_ref[...] = jnp.where(visible, 0.0, -1e30)

    def own_out(head):
        across = sum_ref[row(head), :]
        weight = jnp.exp(spread_ref[head] - across + bias_ref[...])
        weight_ref[head] = weight
        score = product((q_ref[:, columns(head)],), (k_ref[:, columns(head)],), NT) * weight * scale
        score_ref[head] = score
        out_ref[head] = product(split(score), (v_ref[:, columns(head)],), NN)

    forward.run(make_ends, lambda chunk: each_head(chunk, own_out))

    norm_ref[side] = jnp.zeros_like(norm_ref[side])

    def whole_out(head):
        reached = product((q_ref[:, columns(head)],), split(state_ref[head]), NN)
        out = out_ref[head] + jnp.exp(spread_ref[head]) * scale * reached
        out_ref[head] = out
        gained = grad_ref[:, columns(head)].astype(F32) * gain_ref[row(head), :]
        norm_ref[side, 0] += out * out
        norm_ref[side, 1] += gained * out

    for chunk in range(share):
        forward.arrive(chunk)
        each_head(chunk, whole_out)

    norm_copies = to_peers(norm_ref, side, side_peers, "head", norm_sems)
    for copy in norm_copies:
        copy.start()
    for copy in norm_copies:
        copy.wait_recv()
    squares, inners = norm_ref[0, 0], norm_ref[0, 1]
    for place in range(1, split_heads):
        squares, inners = squares + norm_ref[place, 0], inners + norm_ref[place, 1]
    rms = jnp.sqrt(jnp.sum(squares, axis=1, keepdims=True) / full_width + EPS)
    bent = jnp.sum(inners, axis=1, keepdims=True) / (full_width * rms * rms * rms)
    scale_ref[0] = jnp.broadcast_to(1.0 / rms, (length, DK))
    scale_ref[1] = jnp.broadcast_to(bent, (length, DK))

    def own_start(head):
        gained = grad_ref[:, columns(head)].astype(F32) * gain_ref[row(head), :]
        adjoint = gained * scale_ref[0] - out_ref[head] * scale_ref[1]
        adjoint_ref[head] = adjoint
        weighted = adjoint * jnp.exp(spread_ref[head]) * scale
        start_ref[head] = product((q_ref[:, columns(head)],), split(weighted), TN)

    def result(head):
        normed = out_ref[head] * scale_ref[0]
        y_ref[:, columns(head)] = (normed * gain_ref[row(head), :]).astype(BF16)
        grads = grad_ref[:, columns(head)].astype(F32)
        gain_ref_in[inner, row(head), :] = jnp.sum(grads * normed, axis=0, keepdims=True)

    gain_copies_in = to_peers(gain_ref_in, inner, inner_peers, "tm", gain_sems_in)

    def own_grads(head):
        queries, keys = q_ref[:, columns(head)], k_ref[:, columns(head)]
        adjoint = split(adjoint_ref[head])
        pairs = split(product(adjoint, (v_ref[:, columns(head)],), NT) * weight_ref[head])
        reached = product(adjoint, split(state_ref[head]), NT) * jnp.exp(spread_ref[head])
        q_grad = (product(pairs, (keys,), NN) + reached) * scale
        q_grad_ref[:, columns(head)] = q_grad.astype(BF16)
        k_part_ref[head] = product(pairs, (queries,), TN) * scale
        v_part_ref[head] = product(split(score_ref[head]), adjoint, TN)

    def beside(chunk):
        each_head(chunk, result)
        each_head(chunk, own_grads)

    backward.run(lambda chunk: each_head(chunk, own_start), beside)
    stores[0].start()
    for copy in gain_copies_in:
        copy.start()
    stores[1].start()

    for copy in gain_copies_in:
        copy.wait_recv()
    gain_sum = gain_ref_in[0]
    for place in range(1, group):
        gain_sum = gain_sum + gain_ref_in[place]
    gain_ref_out[outer] = gain_sum
    gain_copies_out = to_peers(gain_ref_out, outer, outer_peers, "tm", gain_sems_out)
    for copy in gain_copies_out:
        copy.start()

    ones = jnp.ones((16, DK), BF16)
    ends_here = rows_at == length - 1

    def whole_grads(head):
        later = later_ref[head]
        parts = split(later)
        keys = k_ref[:, columns(head)]
        tail = jnp.exp(total_ref[row(head), :] - spread_ref[head])
        k_grad = k_part_ref[head] + tail * product((v_ref[:, columns(head)],), parts, NT)
        v_grad = v_part_ref[head] + tail * product((keys,), parts, NN)
        k_grad_ref[:, columns(head)] = k_grad.astype(BF16)
        v_grad_ref[:, columns(head)] = v_grad.astype(BF16)
        after = state_ref[head] * jnp.exp(total_ref[row(head), :]) + end_ref[head]
        at_end = jnp.sum(after * later, axis=0, keepdims=True)
        change = out_ref[head] * adjoint_ref[head] - keys.astype(F32) * k_grad
        change = change + jnp.where(ends_here, at_end, 0.0)
        change_ref[row(head), :] = product((ones,), split(change, 3), NT)[:1]

    for chunk in range(share):
        backward.arrive(chunk)
        each_head(chunk, whole_grads)
    stores[2].start()
    stores[3].start()
    from_here = jnp.where(rows_at >= lanes_at, 1.0, 0.0).astype(BF16)
    decay_grad_ref[...] = product(split(change_ref[...], 3), (from_here,), NN)
    stores[4].start()

    for copy in gain_copies_out:
        copy.wait_recv()
    gain_sum = gain_ref_out[0]
    for place in range(1, chain):
        gain_sum = gain_sum + gain_ref_out[place]
    gain_grad_ref[...] = gain_sum
    stores[5].start()

    forward.finish()
    backward.finish()
    for copy in factor_copies + norm_copies + gain_copies_in + gain_copies_out:
        copy.wait_send()
    for store in stores:
        store.wait()


def writer(count, *refs):
    sources, targets, between, sems = refs[:count], refs[count : 2 * count], refs[2 * count : -1], refs[-1]
    steps = [
        (
            pltpu.make_async_copy(sources[number], between[number], sems.at[0, number]),
            pltpu.make_async_copy(between[number], targets[number], sems.at[1, number]),
        )
        for number in range(count)
    ]
    for load, _ in steps:
        load.start()
    for load, store in steps:
        load.wait()
        store.start()
    for _, store in steps:
        store.wait()


def body(group, chain, split_heads, queries, keys, values, log_decay, agent_ids, norm_gain, out_grad):
    length, width = queries.shape
    heads = width // DK
    share = heads // group
    state = (DK, DK)
    row_shape = (heads, DK)
    travelling = [
        pltpu.VMEM((heads, *state), F32),
        pltpu.VMEM((group, share, *state), F32),
        pltpu.VMEM((share, *state), F32),
        pltpu.VMEM((share, *state), F32),
        pltpu.VMEM((group, share, *state), F32),
        pltpu.VMEM((heads, *state), F32),
    ]
    per_head = pltpu.VMEM((heads, length, DK), F32)
    peers, others, sides = max(1, group - 1), max(1, chain - 1), max(1, split_heads - 1)
    wide = jax.ShapeDtypeStruct((length, width), BF16)
    outs = pl.pallas_call(
        functools.partial(kernel, group, chain, split_heads),
        out_shape=[
            wide,
            wide,
            wide,
            wide,
            jax.ShapeDtypeStruct((heads, length), F32),
            jax.ShapeDtypeStruct((heads, DK), F32),
        ],
        in_specs=[pl.BlockSpec(memory_space=pltpu.HBM)] * 7,
        out_specs=[pl.BlockSpec(memory_space=pltpu.HBM)] * 6,
        scratch_shapes=[
            *[pltpu.VMEM((length, width), BF16)] * 3,
            pltpu.VMEM((heads, length), F32),
            pltpu.VMEM((1, length), agent_ids.dtype),
            pltpu.VMEM(row_shape, F32),
            pltpu.VMEM((length, width), BF16),
            *[pltpu.VMEM((length, width), BF16)] * 4,
            pltpu.VMEM((heads, length), F32),
            pltpu.VMEM(row_shape, F32),
            pltpu.VMEM(row_shape, F32),
            pltpu.VMEM(row_shape, F32),
            per_head,
            pltpu.VMEM((length, length), F32),
            pltpu.VMEM((group, *row_shape), F32),
            per_head,
            per_head,
            per_head,
            per_head,
            per_head,
            per_head,
            pltpu.VMEM((split_heads, 2, length, DK), F32),
            pltpu.VMEM((2, length, DK), F32),
            pltpu.VMEM(row_shape, F32),
            pltpu.VMEM((group, *row_shape), F32),
            pltpu.VMEM((chain, *row_shape), F32),
            *travelling,
            *travelling,
            pltpu.SemaphoreType.DMA((7,)),
            pltpu.SemaphoreType.DMA((6,)),
            pltpu.SemaphoreType.DMA((2, 2, 2, peers, share)),
            pltpu.SemaphoreType.DMA((2, 2, share)),
            pltpu.SemaphoreType.DMA((2, peers)),
            pltpu.SemaphoreType.DMA((2, sides)),
            pltpu.SemaphoreType.DMA((2, peers)),
            pltpu.SemaphoreType.DMA((2, others)),
        ],
        compiler_params=pltpu.CompilerParams(
            collective_id=0, has_side_effects=True, vmem_limit_bytes=60 * 2**20
        ),
        cost_estimate=pl.CostEstimate(
            flops=heads * 28 * 2 * DK**3,
            bytes_accessed=8 * length * width * 2,
            transcendentals=heads * 5 * DK**2,
        ),
    )(
        queries,
        keys,
        values,
        log_decay,
        agent_ids.reshape(1, length),
        norm_gain.reshape(heads, DK),
        out_grad,
    )
    outs = pl.pallas_call(
        functools.partial(writer, len(outs)),
        out_shape=[jax.ShapeDtypeStruct(out.shape, out.dtype) for out in outs],
        in_specs=[pl.BlockSpec(memory_space=pltpu.HBM)] * 6,
        out_specs=[pl.BlockSpec(memory_space=pltpu.HBM)] * 6,
        scratch_shapes=[pltpu.VMEM(out.shape, out.dtype) for out in outs]
        + [pltpu.SemaphoreType.DMA((2, len(outs)))],
        compiler_params=pltpu.CompilerParams(vmem_limit_bytes=60 * 2**20),
    )(*outs)
    return (*outs[:5], outs[5].reshape(width))


def solution(mesh):
    count, split_heads = mesh.shape["tm"], mesh.shape["head"]

    def placed_body(queries, *rest):
        group = math.gcd(math.gcd(count, queries.shape[1] // DK), 4)
        return body(group, count // group, split_heads, queries, *rest)

    wide = P("tm", "head")
    return jax.shard_map(
        placed_body,
        mesh=mesh,
        in_specs=(wide, wide, wide, P("head", "tm"), P("tm"), P("head"), wide),
        out_specs=(wide, wide, wide, wide, P("head", "tm"), P("head")),
        check_vma=False,
    )
```
